256 devices in a mesh: space: 32 (over y, z_lo, core), edge: 8 (over z_hi, x).
Axes of the slice: x: 4, y: 4, z: 8 (z_hi: 2, z_lo: 4; z = z_hi * 4 + z_lo), core: 2. Of those that a mesh axis runs over, the one named last changes fastest.
Arguments:
- embeddings: bfloat16 [2048, 49, 128], P(('space', 'edge')), may hold values from -6 to 6
- species: int32 [2048], P(('space', 'edge')), may hold values from 0 to 99
- species_gain: float32 [100, 128], replicated, may hold values from 0.5 to 2
- sources: int32 [32768], P(('space', 'edge')), may hold values from 0 to 127
- targets: int32 [32768], P(('space', 'edge')), may hold values from 0 to 63
- counts: int32 [32], P('space'), may hold values from 512 to 1024, as said below
- send_left: int32 [32, 32], P('space'), may hold values from 0 to 63, as said below
- send_right: int32 [32, 32], P('space'), may hold values from 0 to 63, as said below
- rotations: bfloat16 [235, 32768], P(None, ('space', 'edge')), may hold values from -3 to 3
- radial_basis: bfloat16 [32768, 128], P(('space', 'edge')), may hold values from 0 to 1
- weight_radial: bfloat16 [128, 128], replicated, may hold values from -0.5 to 0.5
- weight_zero: bfloat16 [896, 896], replicated, may hold values from -0.1875 to 0.1875
- weight_one_real: bfloat16 [768, 768], replicated, may hold values from -0.15625 to 0.15625
- weight_one_imag: bfloat16 [768, 768], replicated, may hold values from -0.15625 to 0.15625
- weight_two_real: bfloat16 [640, 640], replicated, may hold values from -0.15625 to 0.15625
- weight_two_imag: bfloat16 [640, 640], replicated, may hold values from -0.15625 to 0.15625
- cotangent: bfloat16 [2048, 49, 128], P(('space', 'edge')), may hold values from -6 to 6
Outputs:
- updated: bfloat16 [2048, 49, 128], P(('space', 'edge'))
- grad_embeddings: float32 [2048, 49, 128], P(('space', 'edge'))
- grad_basis: float32 [32768, 128], P(('space', 'edge'))
The draws below stay inside these ranges and needn't reach their ends.
Inputs may be any that keep to these rules, and one draw needn't show every extreme that they name: Each block's live slots are its first counts[b] slots; at least one block has all 1024 slots live. `send_left`: each row holds 32 distinct atom indices of its block. `send_right`: each row holds 32 distinct atom indices of its block.
All inputs are finite; a program needn't handle non-finite values.
Results may differ from the reference program's by a relative error of at most 0.0065.
Values may be sent and summed in bfloat16 or wider, within the bound.
No kernel may reach another device: no remote copies, remote signals or barrier semaphores. Data moves between devices by JAX's collectives and lax.ppermute only.
A program may use at most 128 MiB of HBM per device.

```python
import math
import jax
import jax.numpy as jnp
from jax import lax

C = 128
LMAX = 6
NC = 49
WROWS = 235
NRBF = 128
NSPEC = 100
BLOCK_ATOMS = 64
BLOCK_EDGES = 1024
HALO = 32
ATOMS = 2048
EDGES = 32768
N_SPACE = 32


def draw_counts(key, part):
    lowest = BLOCK_EDGES // 2
    values = jax.random.randint(key, (N_SPACE,), lowest, BLOCK_EDGES + 1)
    chosen = jax.random.randint(jax.random.fold_in(key, 7), (), 0, N_SPACE)
    return jnp.where(lax.iota(jnp.int32, N_SPACE) == chosen, BLOCK_EDGES, values).astype(jnp.int32)


def send_rows(key):
    subkeys = jax.random.split(key, N_SPACE)
    arranged = jax.vmap(lambda single: jax.random.permutation(single, BLOCK_ATOMS))(subkeys)
    return arranged[:, :HALO].astype(jnp.int32)


def draw_send_left(key, part):
    return send_rows(jax.random.fold_in(key, 11))


def draw_send_right(key, part):
    return send_rows(jax.random.fold_in(key, 23))


def draw_sources(key, part):
    picker = jax.random.randint(jax.random.fold_in(key, 31), (EDGES,), 0, 4)
    inner = jax.random.randint(jax.random.fold_in(key, 37), (EDGES,), 0, BLOCK_ATOMS)
    outer = BLOCK_ATOMS + jax.random.randint(jax.random.fold_in(key, 41), (EDGES,), 0, 2 * HALO)
    return jnp.where(picker == 0, outer, inner).astype(jnp.int32)


def touch_ends(drawn, rng, least, high):
    place = [jax.random.randint(jax.random.fold_in(rng, axis), (), 0, length) for axis, length in enumerate(drawn.shape)]
    longest = drawn.shape.index(max(drawn.shape))
    next_to = place[:longest] + [(place[longest] + 1) % drawn.shape[longest]] + place[longest + 1:]
    return drawn.at[tuple(place)].set(least).at[tuple(next_to)].set(high)


def steps_of(stream_key, dims, cuts, low, largest):
    loudness, own = 1.0, jax.random.fold_in(stream_key, 6)
    for position, shards_of in cuts:
        draws = jnp.exp(jax.random.uniform(jax.random.fold_in(own, position), (shards_of,), jnp.float32, low / len(cuts), largest / len(cuts)))
        loudness = loudness * jnp.repeat(draws, dims[position] // shards_of).reshape([-1 if axis == position else 1 for axis in range(len(dims))])
    return loudness


def gaussian(own_key, extent, deviation, reach, cuts=(), held_as=jnp.bfloat16):
    values = deviation * jax.random.normal(own_key, extent, jnp.float32)
    if cuts:
        values = values * steps_of(own_key, extent, cuts, -0.22, 0.18)
    return jnp.clip(values, -reach, reach).astype(held_as)


def setup_inputs(seed: int = 0) -> dict:
    arg_keys = jax.random.split(jax.random.key(seed), 18)
    embeddings = gaussian(arg_keys[0], (ATOMS, NC, C), 1.0, 6.0, ((0, 256),))
    species = touch_ends(jax.random.randint(arg_keys[1], (ATOMS,), 0, NSPEC), jax.random.fold_in(arg_keys[1], 1), 0, NSPEC - 1).astype(jnp.int32)
    species_gain = jnp.clip(jax.random.uniform(arg_keys[2], (NSPEC, C), jnp.float32, 0.5, 2.0), 0.5, 2.0)
    sources = draw_sources(jax.random.fold_in(arg_keys[17], 71), 0)
    targets = touch_ends(jax.random.randint(arg_keys[4], (EDGES,), 0, BLOCK_ATOMS), jax.random.fold_in(arg_keys[4], 1), 0, BLOCK_ATOMS - 1).astype(jnp.int32)
    counts = draw_counts(jax.random.fold_in(arg_keys[17], 71), 0)
    send_left = draw_send_left(jax.random.fold_in(arg_keys[17], 71), 0)
    send_right = draw_send_right(jax.random.fold_in(arg_keys[17], 71), 0)
    rotations = gaussian(arg_keys[8], (WROWS, EDGES), 0.5, 3.0, ((1, 256),))
    radial_basis = jnp.clip(1.0 * jax.random.uniform(arg_keys[9], (EDGES, NRBF), jnp.float32) ** steps_of(arg_keys[9], (EDGES, NRBF), ((0, 256),), -0.2, 0.2), 0.0, 1.0).astype(jnp.bfloat16)
    weight_radial = gaussian(arg_keys[10], (NRBF, C), NRBF ** -0.5, 0.5)
    weight_zero = gaussian(arg_keys[11], ((LMAX + 1) * C, (LMAX + 1) * C), ((LMAX + 1) * C) ** -0.5, 0.1875)
    weight_one_real = gaussian(arg_keys[12], (LMAX * C, LMAX * C), (2 * LMAX * C) ** -0.5, 0.15625)
    weight_one_imag = gaussian(arg_keys[13], (LMAX * C, LMAX * C), (2 * LMAX * C) ** -0.5, 0.15625)
    weight_two_real = gaussian(arg_keys[14], ((LMAX - 1) * C, (LMAX - 1) * C), (2 * (LMAX - 1) * C) ** -0.5, 0.15625)
    weight_two_imag = gaussian(arg_keys[15], ((LMAX - 1) * C, (LMAX - 1) * C), (2 * (LMAX - 1) * C) ** -0.5, 0.15625)
    cotangent = gaussian(arg_keys[16], (ATOMS, NC, C), 1.0, 6.0, ((0, 256),))
    return dict(embeddings=embeddings, species=species, species_gain=species_gain, sources=sources, targets=targets, counts=counts, send_left=send_left, send_right=send_right, rotations=rotations, radial_basis=radial_basis, weight_radial=weight_radial, weight_zero=weight_zero, weight_one_real=weight_one_real, weight_one_imag=weight_one_imag, weight_two_real=weight_two_real, weight_two_imag=weight_two_imag, cotangent=cotangent)


MOMENTS = (0, 1, -1, 2, -2)

def structure(coefficients):
    top_degree = math.isqrt(coefficients) - 1
    result = []
    offset = 0
    for degree in range(top_degree + 1):
        order_cap = min(degree, 2)
        rows_kept = 2 * order_cap + 1
        result.append((degree, order_cap, rows_kept, offset))
        offset += rows_kept * (2 * degree + 1)
    return result

def rotation_blocks(rotations, coefficients):
    blocks = []
    edge_total = rotations.shape[1]
    for degree, order_cap, rows_kept, offset in structure(coefficients):
        columns = 2 * degree + 1
        blocks.append(rotations[offset:offset + rows_kept * columns].reshape(rows_kept, columns, edge_total))
    return blocks

def rotate_into(blocks, values):
    pieces = []
    for degree, rotation in enumerate(blocks):
        window = values[:, degree * degree:(degree + 1) * (degree + 1), :]
        pieces.append(jnp.einsum('ije,ejc->eic', rotation.astype(jnp.float32), window.astype(jnp.float32)))
    return pieces

def rotate_back(blocks, pieces):
    outcome = [jnp.einsum('ije,eic->ejc', rotation.astype(jnp.float32), fragment.astype(jnp.float32)) for rotation, fragment in zip(blocks, pieces)]
    return jnp.concatenate(outcome, axis=1)

def split_orders(pieces):
    result = []
    for moment in MOMENTS:
        picked = []
        for fragment in pieces:
            center = (fragment.shape[1] - 1) // 2
            if center >= abs(moment):
                picked.append(fragment[:, center + moment])
        result.append(jnp.stack(picked, axis=1))
    return tuple(result)

def join_orders(orders):
    pieces = []
    for degree in range(orders[0].shape[1]):
        order_cap = min(degree, 2)
        picked = [orders[MOMENTS.index(moment)][:, degree - abs(moment)] for moment in range(-order_cap, order_cap + 1)]
        pieces.append(jnp.stack(picked, axis=1))
    return pieces

def flatten(matrix):
    return matrix.reshape(matrix.shape[0], -1)

def product(left_side, right_side):
    return jnp.dot(left_side, right_side, preferred_element_type=jnp.float32)

def product_transposed(left_side, right_side):
    return lax.dot_general(left_side, right_side, (((1,), (1,)), ((), ())), preferred_element_type=jnp.float32)

def frame_mix(orders, weights):
    order_zero, one_up, one_down, two_up, two_down = [flatten(fragment) for fragment in orders]
    weight_zero, one_real, one_imag, two_real, two_imag = weights
    result = (product(order_zero, weight_zero), product(one_up, one_real) - product(one_down, one_imag), product(one_down, one_real) + product(one_up, one_imag), product(two_up, two_real) - product(two_down, two_imag), product(two_down, two_real) + product(two_up, two_imag))
    return tuple((fragment.reshape(initial.shape) for fragment, initial in zip(result, orders)))

def frame_mix_transposed(grads, weights):
    order_zero, one_up, one_down, two_up, two_down = [flatten(fragment) for fragment in grads]
    weight_zero, one_real, one_imag, two_real, two_imag = weights
    result = (product_transposed(order_zero, weight_zero), product_transposed(one_up, one_real) + product_transposed(one_down, one_imag), product_transposed(one_down, one_real) - product_transposed(one_up, one_imag), product_transposed(two_up, two_real) + product_transposed(two_down, two_imag), product_transposed(two_down, two_real) - product_transposed(two_up, two_imag))
    return tuple((fragment.reshape(initial.shape) for fragment, initial in zip(result, grads)))

def gating_forward(outputs):
    scalar = outputs[0][:, 0, :]
    gating = jax.nn.sigmoid(scalar)
    leading = jnp.concatenate([jax.nn.silu(scalar)[:, None, :], outputs[0][:, 1:, :] * gating[:, None, :]], axis=1)
    return (leading,) + tuple((fragment * gating[:, None, :] for fragment in outputs[1:]))

def gating_backward(grads, outputs):
    scalar = outputs[0][:, 0, :]
    gating = jax.nn.sigmoid(scalar)
    gate_slope = gating * (1.0 - gating)
    weighted = sum((lax.optimization_barrier(jnp.sum(upstream * output_part, axis=1)) for upstream, output_part in zip(grads, outputs)))
    lead_grad = grads[0][:, 0, :]
    grad_scalar = lead_grad * (gating + scalar * gate_slope) + gate_slope * (weighted - lead_grad * scalar)
    leading = jnp.concatenate([grad_scalar[:, None, :], grads[0][:, 1:, :] * gating[:, None, :]], axis=1)
    return (leading,) + tuple((upstream * gating[:, None, :] for upstream in grads[1:]))

def forward_edges(gathered, live_mask, blocks, basis_rows, weight_radial, weights):
    turned = split_orders(rotate_into(blocks, gathered))
    radial_pre = product(basis_rows, weight_radial)
    radial = jax.nn.silu(radial_pre)
    scaled = tuple(((fragment * radial[:, None, :]).astype(jnp.bfloat16) for fragment in turned))
    outputs = frame_mix(scaled, weights)
    gated = tuple((fragment.astype(jnp.bfloat16) for fragment in gating_forward(outputs)))
    messages = (rotate_back(blocks, join_orders(gated)) * live_mask[:, None, None]).astype(jnp.bfloat16)
    return (messages, (turned, radial_pre, radial, outputs))

def backward_edges(kept_state, grad_messages, blocks, weight_radial, weights):
    turned, radial_pre, radial, outputs = kept_state
    grad_gated = split_orders(rotate_into(blocks, grad_messages))
    grad_outputs = tuple((fragment.astype(jnp.bfloat16) for fragment in gating_backward(grad_gated, outputs)))
    grad_scaled = frame_mix_transposed(grad_outputs, weights)
    grad_radial = sum((lax.optimization_barrier(jnp.sum(upstream * fragment, axis=1)) for upstream, fragment in zip(grad_scaled, turned)))
    radial_gate = jax.nn.sigmoid(radial_pre)
    grad_pre = (grad_radial * (radial_gate * (1.0 + radial_pre * (1.0 - radial_gate)))).astype(jnp.bfloat16)
    grad_basis = product_transposed(grad_pre, weight_radial)
    grad_turned = tuple(((upstream * radial[:, None, :]).astype(jnp.bfloat16) for upstream in grad_scaled))
    grad_gathered = rotate_back(blocks, join_orders(grad_turned))
    return (grad_gathered, grad_basis)

def reference(embeddings, species, species_gain, sources, targets, counts, send_left, send_right, rotations, radial_basis, weight_radial, weight_zero, weight_one_real, weight_one_imag, weight_two_real, weight_two_imag, cotangent):
    weights = (weight_zero, weight_one_real, weight_one_imag, weight_two_real, weight_two_imag)
    degree_scale = (BLOCK_ATOMS / BLOCK_EDGES) ** 0.5
    block_embed = embeddings.reshape(N_SPACE, BLOCK_ATOMS, NC, C)
    take_rows = jax.vmap(lambda source_rows, indices: jnp.take(source_rows, indices, axis=0))
    from_left = take_rows(jnp.roll(block_embed, 1, axis=0), jnp.roll(send_right, 1, axis=0))
    from_right = take_rows(jnp.roll(block_embed, -1, axis=0), jnp.roll(send_left, -1, axis=0))
    tables = jnp.concatenate([block_embed, from_left, from_right], axis=1)
    onehot = (species[:, None] == lax.iota(jnp.int32, NSPEC)[None, :]).astype(jnp.float32)
    gain_rows = jnp.dot(onehot, species_gain, precision=lax.Precision.HIGHEST)
    grad_aggregate = (cotangent.astype(jnp.float32) * gain_rows[:, None, :] * degree_scale).astype(jnp.bfloat16)
    rotation_parts = rotations.reshape(WROWS, N_SPACE, BLOCK_EDGES).transpose(1, 0, 2)

    def per_block(inputs):
        row_table, source_ids, target_ids, live_count, rotation_part, basis_rows, grad_block = inputs
        live_mask = (lax.iota(jnp.int32, BLOCK_EDGES) < live_count).astype(jnp.float32)
        blocks = rotation_blocks(rotation_part, NC)
        gathered = jnp.take(row_table, source_ids, axis=0)
        messages, kept_state = forward_edges(gathered, live_mask, blocks, basis_rows, weight_radial, weights)
        aggregate = jax.ops.segment_sum(messages.astype(jnp.float32), target_ids, num_segments=BLOCK_ATOMS)
        grad_messages = jnp.take(grad_block, target_ids, axis=0) * live_mask[:, None, None].astype(jnp.bfloat16)
        grad_gathered, grad_basis = backward_edges(kept_state, grad_messages, blocks, weight_radial, weights)
        partial_value = jax.ops.segment_sum(grad_gathered, source_ids, num_segments=BLOCK_ATOMS + 2 * HALO)
        return (aggregate, partial_value, grad_basis)
    aggregate, partial_value, grad_basis = lax.map(per_block, (tables, sources.reshape(N_SPACE, BLOCK_EDGES), targets.reshape(N_SPACE, BLOCK_EDGES), counts, rotation_parts, radial_basis.reshape(N_SPACE, BLOCK_EDGES, NRBF), grad_aggregate.reshape(N_SPACE, BLOCK_ATOMS, NC, C)))
    aggregate = aggregate.reshape(ATOMS, NC, C)
    updated = (embeddings.astype(jnp.float32) + gain_rows[:, None, :] * degree_scale * aggregate).astype(jnp.bfloat16)
    own_rows = partial_value[:, :BLOCK_ATOMS]
    home_right = jnp.roll(partial_value[:, BLOCK_ATOMS:BLOCK_ATOMS + HALO], -1, axis=0)
    home_left = jnp.roll(partial_value[:, BLOCK_ATOMS + HALO:], 1, axis=0)
    add_rows = jax.vmap(lambda source_rows, indices, extras: source_rows.at[indices].add(extras))
    own_rows = add_rows(add_rows(own_rows, send_right, home_right), send_left, home_left)
    grad_embeddings = cotangent.astype(jnp.float32) + own_rows.reshape(ATOMS, NC, C)
    return (updated, grad_embeddings, grad_basis.reshape(EDGES, NRBF))
```

```python
import numpy as np

import jax
import jax.numpy as jnp
from jax import lax
from jax.experimental import pallas as pl
from jax.experimental.pallas import tpu as pltpu
from jax.sharding import PartitionSpec as P

F32 = jnp.float32
BF16 = jnp.bfloat16
LANES = 128
GROUP = 16
TOP = 6
COEFS = (TOP + 1) ** 2
ORDERS = 29
WIDE = COEFS * LANES
VMEM = 50 * 2**20

TILES = ((0, 1, 2, 3), (4,), (5,), (6,))


def place_of(degree, order):
    if order == 0:
        return degree
    start = {1: 7, -1: 13, 2: 19, -2: 24}[order]
    return start + degree - abs(order)


def tile_table():
    table = []
    row_start = 0
    for degrees in TILES:
        first = degrees[0] ** 2
        coefs = (degrees[-1] + 1) ** 2 - first
        pairs = [(d, m) for d in degrees for m in range(-min(d, 2), min(d, 2) + 1)]
        table.append((first, coefs, pairs, row_start))
        row_start += GROUP * len(pairs)
    return table, row_start


TABLE, TURN_ROWS = tile_table()
BACK_ROWS = GROUP * COEFS
ROT_ROWS = 235
ROT_PAD = 256


def selectors():
    pick_turn = np.zeros((TURN_ROWS, ROT_PAD), np.float32)
    pick_back = np.zeros((BACK_ROWS, ROT_PAD), np.float32)
    mask_turn = np.zeros((ROT_PAD, 256), np.float32)
    mask_back = np.zeros((ROT_PAD, 256), np.float32)
    offset = 0
    for degree in range(TOP + 1):
        cap = min(degree, 2)
        [(first, _, pairs, start)] = [
            e for e, d in zip(TABLE, TILES) if degree in d
        ]
        for order in range(-cap, cap + 1):
            row_block = pairs.index((degree, order))
            for column in range(2 * degree + 1):
                row = offset + (order + cap) * (2 * degree + 1) + column
                coef = degree * degree + column
                pick_turn[start + GROUP * row_block : start + GROUP * (row_block + 1), row] = 1
                pick_back[GROUP * coef : GROUP * (coef + 1), row] = 1
                mask_turn[row, GROUP * (coef - first) : GROUP * (coef - first + 1)] = 1
                mask_back[row, GROUP * row_block : GROUP * (row_block + 1)] = 1
        offset += (2 * cap + 1) * (2 * degree + 1)
    return pick_turn, pick_back, mask_turn, mask_back


def dot(a, b):
    return jnp.dot(a, b, preferred_element_type=F32)


def dot_nt(a, b):
    return lax.dot_general(a, b, (((1,), (1,)), ((), ())), preferred_element_type=F32)


def chunks(total, size):
    return [(s, min(size, total - s)) for s in range(0, total, size)]


def prep_kernel(rot, pick_turn, pick_back, mask_turn, mask_back, turn, back):
    row = lax.broadcasted_iota(jnp.int32, (LANES, 256), 0)
    lane = lax.broadcasted_iota(jnp.int32, (LANES, 256), 1) & (GROUP - 1)

    def keep(rows):
        r = lax.broadcasted_iota(jnp.int32, (rows, 256), 0) & (GROUP - 1)
        c = lax.broadcasted_iota(jnp.int32, (rows, 256), 1) & (GROUP - 1)
        return r == c

    keep_turn, keep_back = keep(TURN_ROWS), keep(BACK_ROWS)
    for g in range(LANES // GROUP):
        spread = (row == lane + GROUP * g).astype(F32).astype(BF16)
        laid = dot(rot[...], spread)
        for mask, pick, kept, out in (
            (mask_turn, pick_turn, keep_turn, turn),
            (mask_back, pick_back, keep_back, back),
        ):
            full = dot(pick[...], (laid * mask[...]).astype(BF16))
            out[g] = jnp.where(kept, full, 0.0).astype(BF16)


def rotate(turn, wide, use):
    for g in range(LANES // GROUP):
        rows = pl.ds(GROUP * g, GROUP)
        for first, coefs, pairs, start in TABLE:
            window = jnp.concatenate(
                [wide[rows, pl.ds((first + c) * LANES, LANES)] for c in range(coefs)], axis=0
            )
            block = turn[g, pl.ds(start, GROUP * len(pairs)), pl.ds(0, GROUP * coefs)]
            result = dot(block, window)
            for k, (degree, order) in enumerate(pairs):
                use(g, degree, order, result[GROUP * k : GROUP * (k + 1)])


def rotate_back(back, fragments, wide):
    for g in range(LANES // GROUP):
        rows = pl.ds(GROUP * g, GROUP)
        for first, coefs, pairs, _ in TABLE:
            window = jnp.concatenate(
                [fragments[rows, pl.ds(place_of(*p) * LANES, LANES)] for p in pairs], axis=0
            )
            block = back[g, pl.ds(GROUP * first, GROUP * coefs), pl.ds(0, GROUP * len(pairs))]
            result = dot(block, window)
            for c in range(coefs):
                wide[rows, pl.ds((first + c) * LANES, LANES)] = result[
                    GROUP * c : GROUP * (c + 1)
                ].astype(BF16)


def pick_rows(ids, pieces, wide):
    total = sum(p.shape[0] for p in pieces)
    hot = (ids[...] == lax.broadcasted_iota(jnp.int32, (LANES, total), 1)).astype(F32).astype(BF16)
    for start, size in chunks(WIDE, 256):
        lanes = pl.ds(start, size)
        table = jnp.concatenate([p[:, lanes] for p in pieces], axis=0)
        wide[:, lanes] = dot(hot, table).astype(BF16)


def add_rows(ids, wide, pieces):
    total = sum(p.shape[0] for p in pieces)
    hot = (ids[...] == lax.broadcasted_iota(jnp.int32, (total, LANES), 0)).astype(F32).astype(BF16)
    for start, size in chunks(WIDE, 256):
        lanes = pl.ds(start, size)
        summed = dot(hot, wide[:, lanes]).astype(BF16)
        offset = 0
        for p in pieces:
            p[:, lanes] = summed[offset : offset + p.shape[0]]
            offset += p.shape[0]


def put_order(zero, one, two, g, degree, order, value):
    where, lead = {0: (zero, 0), 1: (one, 1), 2: (two, 2)}[abs(order)]
    base = LANES if order < 0 else 0
    where[pl.ds(base + GROUP * g, GROUP), pl.ds((degree - lead) * LANES, LANES)] = value


def forward_kernel(
    own, partner, far0, far1, far2, far3, src, tgt, turn, back, basis, w_rad, w0, w1r, w1i, w2r, w2i,
    agg0, agg1, agg2, agg3, turned, outs, pre,
    wide, zero, one, two, gated, rad,
):
    value = dot(basis[...], w_rad[...])
    pre[...] = value
    rad[...] = value * jax.nn.sigmoid(value)
    pick_rows(src, (own, partner, far0, far1, far2, far3), wide)

    def use(g, degree, order, part):
        rows = pl.ds(GROUP * g, GROUP)
        turned[rows, pl.ds(place_of(degree, order) * LANES, LANES)] = part
        put_order(zero, one, two, g, degree, order, (part * rad[rows, :]).astype(BF16))

    rotate(turn, wide, use)
    for start, size in chunks(7 * LANES, 256):
        outs[:, pl.ds(start, size)] = dot(zero[...], w0[:, pl.ds(start, size)])
    for stacked, real, imag, up, down, count in (
        (one, w1r, w1i, 7, 13, 6),
        (two, w2r, w2i, 19, 24, 5),
    ):
        for start, size in chunks(count * LANES, 256):
            a = dot(stacked[...], real[:, pl.ds(start, size)])
            b = dot(stacked[...], imag[:, pl.ds(start, size)])
            outs[:, pl.ds(up * LANES + start, size)] = a[:LANES] - b[LANES:]
            outs[:, pl.ds(down * LANES + start, size)] = a[LANES:] + b[:LANES]
    gate = jax.nn.sigmoid(outs[:, pl.ds(0, LANES)])
    for q in range(ORDERS):
        lanes = pl.ds(q * LANES, LANES)
        gated[:, lanes] = (outs[:, lanes] * gate).astype(BF16)
    rotate_back(back, gated, wide)
    add_rows(tgt, wide, (agg0, agg1, agg2, agg3))


def backward_kernel(
    up0, up1, up2, up3, tgt, src, turn, back, turned, outs, pre, w_rad, w0, w1r, w1i, w2r, w2i,
    own, partner, far0, far1, far2, far3, grad_basis,
    wide, zero, one, two, grads, rad,
):
    pick_rows(tgt, (up0, up1, up2, up3), wide)

    def use(g, degree, order, part):
        grads[pl.ds(GROUP * g, GROUP), pl.ds(place_of(degree, order) * LANES, LANES)] = part

    rotate(turn, wide, use)
    scalar = outs[:, pl.ds(0, LANES)]
    gate = jax.nn.sigmoid(scalar)
    slope = gate * (1.0 - gate)
    lead = grads[:, pl.ds(0, LANES)]
    weighted = lead * scalar
    for q in range(1, ORDERS):
        lanes = pl.ds(q * LANES, LANES)
        weighted = weighted + grads[:, lanes] * outs[:, lanes]
    zero[:, pl.ds(0, LANES)] = (
        lead * (gate + scalar * slope) + slope * (weighted - lead * scalar)
    ).astype(BF16)
    for stacked, count, base, q0 in ((zero, 6, 0, 1), (one, 6, 0, 7), (one, 6, LANES, 13), (two, 5, 0, 19), (two, 5, LANES, 24)):
        for k in range(count):
            value = (grads[:, pl.ds((q0 + k) * LANES, LANES)] * gate).astype(BF16)
            column = k + 1 if stacked is zero else k
            stacked[pl.ds(base, LANES), pl.ds(column * LANES, LANES)] = value
    value = pre[...]
    gate = jax.nn.sigmoid(value)
    rad[...] = value * gate
    slope = gate * (1.0 + value * (1.0 - gate))
    total = jnp.zeros((LANES, LANES), F32)

    def take(total, q, scaled):
        lanes = pl.ds(q * LANES, LANES)
        wide[:, lanes] = (scaled * rad[...]).astype(BF16)
        return total + scaled * turned[:, lanes]

    for start, size in chunks(7 * LANES, 256):
        a = dot_nt(zero[...], w0[pl.ds(start, size), :])
        for k in range(size // LANES):
            total = take(total, start // LANES + k, a[:, k * LANES : (k + 1) * LANES])
    for stacked, real, imag, up, down, count in (
        (one, w1r, w1i, 7, 13, 6),
        (two, w2r, w2i, 19, 24, 5),
    ):
        for start, size in chunks(count * LANES, 256):
            a = dot_nt(stacked[...], real[pl.ds(start, size), :])
            b = dot_nt(stacked[...], imag[pl.ds(start, size), :])
            for k in range(size // LANES):
                cut = slice(k * LANES, (k + 1) * LANES)
                total = take(total, up + start // LANES + k, a[:LANES, cut] + b[LANES:, cut])
                total = take(total, down + start // LANES + k, a[LANES:, cut] - b[:LANES, cut])
    grad_basis[...] = dot_nt((total * slope).astype(BF16), w_rad[...])
    for q in range(ORDERS):
        lanes = pl.ds(q * LANES, LANES)
        zero_q = wide[:, lanes]
        grads[:, lanes] = zero_q.astype(F32)
    rotate_back_f32(back, grads, wide)
    add_rows(src, wide, (own, partner, far0, far1, far2, far3))


def rotate_back_f32(back, fragments, wide):
    for g in range(LANES // GROUP):
        rows = pl.ds(GROUP * g, GROUP)
        for first, coefs, pairs, _ in TABLE:
            window = jnp.concatenate(
                [fragments[rows, pl.ds(place_of(*p) * LANES, LANES)] for p in pairs], axis=0
            ).astype(BF16)
            block = back[g, pl.ds(GROUP * first, GROUP * coefs), pl.ds(0, GROUP * len(pairs))]
            result = dot(block, window)
            for c in range(coefs):
                wide[rows, pl.ds((first + c) * LANES, LANES)] = result[
                    GROUP * c : GROUP * (c + 1)
                ].astype(BF16)


def kernel_call(kernel, outs, scratch, flops, moved):
    return pl.pallas_call(
        kernel,
        out_shape=outs,
        scratch_shapes=scratch,
        compiler_params=pltpu.CompilerParams(vmem_limit_bytes=VMEM),
        cost_estimate=pl.CostEstimate(flops=flops, bytes_accessed=moved, transcendentals=0),
    )


def shaped(*dims, kind=BF16):
    return jax.ShapeDtypeStruct(dims, kind)


def on_device(
    embeddings, species, species_gain, sources, targets, counts, send_left, send_right, rotations,
    radial_basis, weight_radial, weight_zero, weight_one_real, weight_one_imag, weight_two_real,
    weight_two_imag, cotangent,
):
    weights = (weight_zero, weight_one_real, weight_one_imag, weight_two_real, weight_two_imag)
    atoms = embeddings.shape[0]
    edges = sources.shape[0]
    blocks = lax.axis_size("space")
    member = lax.axis_index("edge")
    block = lax.axis_index("space")
    half, along = member // 4, member % 4
    odd = block % 2
    scale = (atoms / edges) ** 0.5

    def across(v):
        return lax.ppermute(v, "edge", [(s, (s + 4) % 8) for s in range(8)])

    def shift(v, k):
        return lax.ppermute(v, "edge", [(s, s // 4 * 4 + (s + k) % 4) for s in range(8)])

    def swap_near(v):
        return lax.ppermute(v, "space", [(b, b ^ 1) for b in range(blocks)])

    def swap_far(v):
        return lax.ppermute(v, "space", [(b, (b + 2 * (b % 2) - 1) % blocks) for b in range(blocks)])

    def roll(v, k):
        return lax.ppermute(v, "space", [(b, (b + k) % blocks) for b in range(blocks)])

    def spread(v):
        return [v] + [shift(v, 4 - d) for d in (1, 2, 3)]

    def collect(parts):
        total = parts[0].astype(F32)
        for d in (1, 2, 3):
            total = total + shift(parts[d], d).astype(F32)
        return total

    gain = jnp.dot(
        (species[:, None] == lax.iota(jnp.int32, species_gain.shape[0])[None, :]).astype(F32),
        species_gain,
        precision=lax.Precision.HIGHEST,
    )
    flat = embeddings.reshape(atoms, WIDE)
    upstream = (cotangent.astype(F32) * gain[:, None, :] * scale).astype(BF16).reshape(atoms, WIDE)

    pair = jnp.concatenate([flat, across(flat)], axis=0)
    far_pair = swap_far(pair)
    own_pieces = spread(pair)
    own_table = jnp.concatenate(own_pieces, axis=0)
    partner_table = swap_near(own_table)
    far_pieces = spread(far_pair)
    up_pair = jnp.concatenate([upstream, across(upstream)], axis=0)
    up_pieces = spread(up_pair)

    def slot(atom):
        owner, row = atom // atoms, atom % atoms
        return (owner % 4 - along) % 4 * (2 * atoms) + (owner // 4 - half) % 2 * atoms + row

    lists = jnp.concatenate([roll(send_right, 1), roll(send_left, -1)], axis=1)[0]
    halo = send_left.shape[1]
    block_atoms = 8 * atoms
    halo_hot = (sources[:, None] - block_atoms) == lax.iota(jnp.int32, 2 * halo)[None, :]
    halo_atom = jnp.sum(jnp.where(halo_hot, lists[None, :], 0), axis=1)
    on_left = sources < block_atoms + halo
    near = jnp.where(on_left, odd == 1, odd == 0)
    src = jnp.where(
        sources < block_atoms,
        slot(sources),
        jnp.where(near, block_atoms, 2 * block_atoms) + slot(halo_atom),
    ).astype(jnp.int32)
    live = member * edges + lax.iota(jnp.int32, edges) < counts[0]
    tgt = jnp.where(live, slot(targets), -1).astype(jnp.int32)
    src_col, src_row = src[:, None], src[None, :]
    tgt_col, tgt_row = tgt[:, None], tgt[None, :]

    pick_turn, pick_back, mask_turn, mask_back = selectors()
    groups = LANES // GROUP
    turn, back = kernel_call(
        prep_kernel,
        (shaped(groups, TURN_ROWS, 256), shaped(groups, BACK_ROWS, 256)),
        [],
        2 * 10**9,
        6 * 10**6,
    )(
        jnp.pad(rotations, ((0, ROT_PAD - ROT_ROWS), (0, 0))),
        jnp.asarray(pick_turn, BF16),
        jnp.asarray(pick_back, BF16),
        jnp.asarray(mask_turn, F32),
        jnp.asarray(mask_back, F32),
    )

    def work():
        return [
            pltpu.VMEM((edges, WIDE), BF16),
            pltpu.VMEM((edges, 7 * LANES), BF16),
            pltpu.VMEM((2 * edges, 6 * LANES), BF16),
            pltpu.VMEM((2 * edges, 5 * LANES), BF16),
        ]

    piece = shaped(2 * atoms, WIDE)
    whole = shaped(block_atoms, WIDE)
    kept = shaped(edges, ORDERS * LANES, kind=F32)
    square = shaped(edges, LANES, kind=F32)
    *aggs, turned, outs, pre = kernel_call(
        forward_kernel,
        (piece, piece, piece, piece, kept, kept, square),
        work() + [pltpu.VMEM((edges, ORDERS * LANES), BF16), pltpu.VMEM((edges, LANES), F32)],
        4 * 10**9,
        20 * 10**6,
    )(own_table, partner_table, *far_pieces, src_col, tgt_row, turn, back, radial_basis, weight_radial, *weights)

    agg_pair = collect(aggs)
    aggregate = agg_pair[:atoms] + across(agg_pair[atoms:].astype(BF16)).astype(F32)
    updated = (
        embeddings.astype(F32) + gain[:, None, :] * scale * aggregate.reshape(embeddings.shape)
    ).astype(BF16)

    own_grad, near_grad, *far_grads, grad_basis = kernel_call(
        backward_kernel,
        (whole, whole, piece, piece, piece, piece, square),
        work() + [pltpu.VMEM((edges, ORDERS * LANES), F32), pltpu.VMEM((edges, LANES), F32)],
        5 * 10**9,
        20 * 10**6,
    )(*up_pieces, tgt_col, src_row, turn, back, turned, outs, pre, weight_radial, *weights)

    far_home = swap_far(collect(far_grads).astype(BF16)).astype(F32)
    summed = own_grad.astype(F32) + swap_near(near_grad).astype(F32)
    parts = [summed[2 * atoms * d : 2 * atoms * (d + 1)].astype(BF16) for d in range(4)]
    grad_pair = collect(parts) + far_home
    grad_rows = grad_pair[:atoms] + across(grad_pair[atoms:].astype(BF16)).astype(F32)
    grad_embeddings = cotangent.astype(F32) + grad_rows.reshape(cotangent.shape)
    return (updated, grad_embeddings, grad_basis)


def solution(mesh):
    both = ("space", "edge")
    placed = (
        P(both, None, None), P(both), P(), P(both), P(both), P("space"), P("space", None),
        P("space", None), P(None, both), P(both, None), P(), P(), P(), P(), P(), P(),
        P(both, None, None),
    )
    return jax.shard_map(
        on_device,
        mesh=mesh,
        in_specs=placed,
        out_specs=(P(both, None, None), P(both, None, None), P(both, None)),
        check_vma=False,
    )
```

```python
import numpy as np

import jax
import jax.numpy as jnp
from jax import lax
from jax.experimental import pallas as pl
from jax.experimental.pallas import tpu as pltpu
from jax.sharding import PartitionSpec as P

F32 = jnp.float32
BF16 = jnp.bfloat16
LANES = 128
GROUP = 16
TOP = 6
COEFS = (TOP + 1) ** 2
ORDERS = 29
WIDE = COEFS * LANES
VMEM = 50 * 2**20

TILES = ((0, 1, 2, 3), (4,), (5,), (6,))


def place_of(degree, order):
    if order == 0:
        return degree
    start = {1: 7, -1: 13, 2: 19, -2: 24}[order]
    return start + degree - abs(order)


def tile_table():
    table = []
    row_start = 0
    for degrees in TILES:
        first = degrees[0] ** 2
        coefs = (degrees[-1] + 1) ** 2 - first
        pairs = [(d, m) for d in degrees for m in range(-min(d, 2), min(d, 2) + 1)]
        table.append((first, coefs, pairs, row_start))
        row_start += GROUP * len(pairs)
    return table, row_start


TABLE, TURN_ROWS = tile_table()
BACK_ROWS = GROUP * COEFS
ROT_ROWS = 235
ROT_PAD = 256


def selectors():
    pair_all, coef_all, pair_tile, coef_tile = [np.full(ROT_PAD, -1, np.int32) for _ in range(4)]
    offset = 0
    for degree in range(TOP + 1):
        cap = min(degree, 2)
        [(first, _, pairs, start)] = [e for e, d in zip(TABLE, TILES) if degree in d]
        for order in range(-cap, cap + 1):
            place = pairs.index((degree, order))
            for column in range(2 * degree + 1):
                row = offset + (order + cap) * (2 * degree + 1) + column
                coef = degree * degree + column
                pair_all[row], coef_all[row] = start // GROUP + place, coef
                pair_tile[row], coef_tile[row] = place, coef - first
        offset += (2 * cap + 1) * (2 * degree + 1)
    return pair_all[None, :], coef_all[None, :], pair_tile[:, None], coef_tile[:, None]


def dot(a, b):
    return jnp.dot(a, b, preferred_element_type=F32)


def dot_nt(a, b):
    return lax.dot_general(a, b, (((1,), (1,)), ((), ())), preferred_element_type=F32)


def chunks(total, size):
    return [(s, min(size, total - s)) for s in range(0, total, size)]


def prep_kernel(rot, pair_all, coef_all, pair_tile, coef_tile, turn, back):
    row = lax.broadcasted_iota(jnp.int32, (LANES, 256), 0)
    lane = lax.broadcasted_iota(jnp.int32, (LANES, 256), 1) & (GROUP - 1)

    def keep(rows):
        r = lax.broadcasted_iota(jnp.int32, (rows, 256), 0) & (GROUP - 1)
        c = lax.broadcasted_iota(jnp.int32, (rows, 256), 1) & (GROUP - 1)
        return r == c

    def pick(rows, ids):
        group = lax.broadcasted_iota(jnp.int32, (rows, ROT_PAD), 0) // GROUP
        return (group == ids[...]).astype(F32).astype(BF16)

    def mask(ids):
        return lax.broadcasted_iota(jnp.int32, (ROT_PAD, 256), 1) // GROUP == ids[...]

    work = (
        (mask(coef_tile), pick(TURN_ROWS, pair_all), keep(TURN_ROWS), turn),
        (mask(pair_tile), pick(BACK_ROWS, coef_all), keep(BACK_ROWS), back),
    )
    for g in range(LANES // GROUP):
        spread = (row == lane + GROUP * g).astype(F32).astype(BF16)
        laid = dot(rot[...], spread)
        for masked, picked, kept, out in work:
            full = dot(picked, jnp.where(masked, laid, 0.0).astype(BF16))
            out[g] = jnp.where(kept, full, 0.0).astype(BF16)


def rotate(turn, wide, use):
    for g in range(LANES // GROUP):
        rows = pl.ds(GROUP * g, GROUP)
        for first, coefs, pairs, start in TABLE:
            window = jnp.concatenate(
                [wide[rows, pl.ds((first + c) * LANES, LANES)] for c in range(coefs)], axis=0
            )
            block = turn[g, pl.ds(start, GROUP * len(pairs)), pl.ds(0, GROUP * coefs)]
            result = dot(block, window)
            for k, (degree, order) in enumerate(pairs):
                use(g, degree, order, result[GROUP * k : GROUP * (k + 1)])


def rotate_back(back, fragments, wide):
    for g in range(LANES // GROUP):
        rows = pl.ds(GROUP * g, GROUP)
        for first, coefs, pairs, _ in TABLE:
            window = jnp.concatenate(
                [fragments[rows, pl.ds(place_of(*p) * LANES, LANES)] for p in pairs], axis=0
            )
            block = back[g, pl.ds(GROUP * first, GROUP * coefs), pl.ds(0, GROUP * len(pairs))]
            result = dot(block, window)
            for c in range(coefs):
                wide[rows, pl.ds((first + c) * LANES, LANES)] = result[
                    GROUP * c : GROUP * (c + 1)
                ].astype(BF16)


def pick_rows(ids, pieces, wide):
    total = sum(p.shape[0] for p in pieces)
    hot = (ids[...] == lax.broadcasted_iota(jnp.int32, (LANES, total), 1)).astype(F32).astype(BF16)
    for start, size in chunks(WIDE, 256):
        lanes = pl.ds(start, size)
        table = jnp.concatenate([p[:, lanes] for p in pieces], axis=0)
        wide[:, lanes] = dot(hot, table).astype(BF16)


def add_rows(ids, wide, pieces):
    total = sum(p.shape[0] for p in pieces)
    hot = (ids[...] == lax.broadcasted_iota(jnp.int32, (total, LANES), 0)).astype(F32).astype(BF16)
    for start, size in chunks(WIDE, 256):
        lanes = pl.ds(start, size)
        summed = dot(hot, wide[:, lanes]).astype(BF16)
        offset = 0
        for p in pieces:
            p[:, lanes] = summed[offset : offset + p.shape[0]]
            offset += p.shape[0]


def put_order(zero, one, two, g, degree, order, value):
    where, lead = {0: (zero, 0), 1: (one, 1), 2: (two, 2)}[abs(order)]
    base = LANES if order < 0 else 0
    where[pl.ds(base + GROUP * g, GROUP), pl.ds((degree - lead) * LANES, LANES)] = value


def forward_kernel(
    own, partner, far0, far1, far2, far3, src, tgt, turn, back, basis, w_rad, w0, w1r, w1i, w2r, w2i,
    agg0, agg1, agg2, agg3, turned, outs, pre,
    wide, zero, one, two, gated, rad,
):
    value = dot(basis[...], w_rad[...])
    pre[...] = value
    rad[...] = value * jax.nn.sigmoid(value)
    pick_rows(src, (own, partner, far0, far1, far2, far3), wide)

    def use(g, degree, order, part):
        rows = pl.ds(GROUP * g, GROUP)
        turned[rows, pl.ds(place_of(degree, order) * LANES, LANES)] = part
        put_order(zero, one, two, g, degree, order, (part * rad[rows, :]).astype(BF16))

    rotate(turn, wide, use)
    for start, size in chunks(7 * LANES, 256):
        outs[:, pl.ds(start, size)] = dot(zero[...], w0[:, pl.ds(start, size)])
    for stacked, real, imag, up, down, count in (
        (one, w1r, w1i, 7, 13, 6),
        (two, w2r, w2i, 19, 24, 5),
    ):
        for start, size in chunks(count * LANES, 256):
            a = dot(stacked[...], real[:, pl.ds(start, size)])
            b = dot(stacked[...], imag[:, pl.ds(start, size)])
            outs[:, pl.ds(up * LANES + start, size)] = a[:LANES] - b[LANES:]
            outs[:, pl.ds(down * LANES + start, size)] = a[LANES:] + b[:LANES]
    gate = jax.nn.sigmoid(outs[:, pl.ds(0, LANES)])
    for q in range(ORDERS):
        lanes = pl.ds(q * LANES, LANES)
        gated[:, lanes] = (outs[:, lanes] * gate).astype(BF16)
    rotate_back(back, gated, wide)
    add_rows(tgt, wide, (agg0, agg1, agg2, agg3))


def backward_kernel(
    up0, up1, up2, up3, tgt, src, turn, back, turned, outs, pre, w_rad, w0, w1r, w1i, w2r, w2i,
    own, partner, far0, far1, far2, far3, grad_basis,
    wide, zero, one, two, grads, fragments, rad,
):
    pick_rows(tgt, (up0, up1, up2, up3), wide)

    def use(g, degree, order, part):
        grads[pl.ds(GROUP * g, GROUP), pl.ds(place_of(degree, order) * LANES, LANES)] = part

    rotate(turn, wide, use)
    scalar = outs[:, pl.ds(0, LANES)]
    gate = jax.nn.sigmoid(scalar)
    slope = gate * (1.0 - gate)
    lead = grads[:, pl.ds(0, LANES)]
    weighted = lead * scalar
    for q in range(1, ORDERS):
        lanes = pl.ds(q * LANES, LANES)
        weighted = weighted + grads[:, lanes] * outs[:, lanes]
    zero[:, pl.ds(0, LANES)] = (
        lead * (gate + scalar * slope) + slope * (weighted - lead * scalar)
    ).astype(BF16)
    for stacked, count, base, q0 in ((zero, 6, 0, 1), (one, 6, 0, 7), (one, 6, LANES, 13), (two, 5, 0, 19), (two, 5, LANES, 24)):
        for k in range(count):
            value = (grads[:, pl.ds((q0 + k) * LANES, LANES)] * gate).astype(BF16)
            column = k + 1 if stacked is zero else k
            stacked[pl.ds(base, LANES), pl.ds(column * LANES, LANES)] = value
    value = pre[...]
    gate = jax.nn.sigmoid(value)
    rad[...] = value * gate
    slope = gate * (1.0 + value * (1.0 - gate))
    total = jnp.zeros((LANES, LANES), F32)

    def take(total, q, scaled):
        lanes = pl.ds(q * LANES, LANES)
        fragments[:, lanes] = (scaled * rad[...]).astype(BF16)
        return total + scaled * turned[:, lanes]

    for start, size in chunks(7 * LANES, 256):
        a = dot_nt(zero[...], w0[pl.ds(start, size), :])
        for k in range(size // LANES):
            total = take(total, start // LANES + k, a[:, k * LANES : (k + 1) * LANES])
    for stacked, real, imag, up, down, count in (
        (one, w1r, w1i, 7, 13, 6),
        (two, w2r, w2i, 19, 24, 5),
    ):
        for start, size in chunks(count * LANES, 256):
            a = dot_nt(stacked[...], real[pl.ds(start, size), :])
            b = dot_nt(stacked[...], imag[pl.ds(start, size), :])
            for k in range(size // LANES):
                cut = slice(k * LANES, (k + 1) * LANES)
                total = take(total, up + start // LANES + k, a[:LANES, cut] + b[LANES:, cut])
                total = take(total, down + start // LANES + k, a[LANES:, cut] - b[:LANES, cut])
    grad_basis[...] = dot_nt((total * slope).astype(BF16), w_rad[...])
    rotate_back(back, fragments, wide)
    add_rows(src, wide, (own, partner, far0, far1, far2, far3))


def kernel_call(kernel, outs, scratch, flops, moved):
    return pl.pallas_call(
        kernel,
        out_shape=outs,
        scratch_shapes=scratch,
        compiler_params=pltpu.CompilerParams(vmem_limit_bytes=VMEM),
        cost_estimate=pl.CostEstimate(flops=flops, bytes_accessed=moved, transcendentals=0),
    )


def shaped(*dims, kind=BF16):
    return jax.ShapeDtypeStruct(dims, kind)


def on_device(
    embeddings, species, species_gain, sources, targets, counts, send_left, send_right, rotations,
    radial_basis, weight_radial, weight_zero, weight_one_real, weight_one_imag, weight_two_real,
    weight_two_imag, cotangent,
):
    weights = (weight_zero, weight_one_real, weight_one_imag, weight_two_real, weight_two_imag)
    atoms = embeddings.shape[0]
    edges = sources.shape[0]
    blocks = lax.axis_size("space")
    member = lax.axis_index("edge")
    block = lax.axis_index("space")
    half, along = member // 4, member % 4
    odd = block % 2
    scale = (atoms / edges) ** 0.5

    def across(v):
        return lax.ppermute(v, "edge", [(s, (s + 4) % 8) for s in range(8)])

    def shift(v, k):
        return lax.ppermute(v, "edge", [(s, s // 4 * 4 + (s + k) % 4) for s in range(8)])

    def swap_near(v):
        return lax.ppermute(v, "space", [(b, b ^ 1) for b in range(blocks)])

    def swap_far(v):
        return lax.ppermute(v, "space", [(b, (b + 2 * (b % 2) - 1) % blocks) for b in range(blocks)])

    def roll(v, k):
        return lax.ppermute(v, "space", [(b, (b + k) % blocks) for b in range(blocks)])

    def after(*values):
        return lax.optimization_barrier(values)

    def spread(v):
        return [v] + [shift(v, 4 - d) for d in (1, 2, 3)]

    def collect(parts):
        total = parts[0].astype(F32)
        for d in (1, 2, 3):
            total = total + shift(parts[d], d).astype(F32)
        return total

    groups = LANES // GROUP
    turn, back = kernel_call(
        prep_kernel,
        (shaped(groups, TURN_ROWS, 256), shaped(groups, BACK_ROWS, 256)),
        [],
        2 * 10**9,
        6 * 10**6,
    )(
        jnp.pad(rotations, ((0, ROT_PAD - ROT_ROWS), (0, 0))),
        *[jnp.asarray(ids) for ids in selectors()],
    )

    flat = embeddings.reshape(atoms, WIDE)
    beyond, turn, back = after(across(flat), turn, back)
    pair = jnp.concatenate([flat, beyond], axis=0)
    pair, species, upstream, targets = after(pair, species, cotangent, targets)
    far_pair = swap_far(pair)
    own_pieces = spread(pair)
    gain = jnp.dot(
        (species[:, None] == lax.iota(jnp.int32, species_gain.shape[0])[None, :]).astype(F32),
        species_gain,
        precision=lax.Precision.HIGHEST,
    )
    upstream = (upstream.astype(F32) * gain[:, None, :] * scale).astype(BF16).reshape(atoms, WIDE)
    up_pair = jnp.concatenate([upstream, across(upstream)], axis=0)
    *own_pieces, send_left, send_right, sources = after(*own_pieces, send_left, send_right, sources)
    own_table = jnp.concatenate(own_pieces, axis=0)
    partner_table = swap_near(own_table)
    far_pieces = spread(far_pair)
    *far_pieces, up_pair = after(*far_pieces, up_pair)
    up_pieces = spread(up_pair)

    def slot(atom):
        owner, row = atom // atoms, atom % atoms
        return (owner % 4 - along) % 4 * (2 * atoms) + (owner // 4 - half) % 2 * atoms + row

    lists = jnp.concatenate([roll(send_right, 1), roll(send_left, -1)], axis=1)[0]
    halo = send_left.shape[1]
    block_atoms = 8 * atoms
    halo_hot = (sources[:, None] - block_atoms) == lax.iota(jnp.int32, 2 * halo)[None, :]
    halo_atom = jnp.sum(jnp.where(halo_hot, lists[None, :], 0), axis=1)
    on_left = sources < block_atoms + halo
    near = jnp.where(on_left, odd == 1, odd == 0)
    src = jnp.where(
        sources < block_atoms,
        slot(sources),
        jnp.where(near, block_atoms, 2 * block_atoms) + slot(halo_atom),
    ).astype(jnp.int32)
    live = member * edges + lax.iota(jnp.int32, edges) < counts[0]
    tgt = jnp.where(live, slot(targets), -1).astype(jnp.int32)
    src_col, src_row = src[:, None], src[None, :]
    tgt_col, tgt_row = tgt[:, None], tgt[None, :]

    def work():
        return [
            pltpu.VMEM((edges, WIDE), BF16),
            pltpu.VMEM((edges, 7 * LANES), BF16),
            pltpu.VMEM((2 * edges, 6 * LANES), BF16),
            pltpu.VMEM((2 * edges, 5 * LANES), BF16),
        ]

    piece = shaped(2 * atoms, WIDE)
    whole = shaped(block_atoms, WIDE)
    kept = shaped(edges, ORDERS * LANES, kind=F32)
    square = shaped(edges, LANES, kind=F32)
    *aggs, turned, outs, pre = kernel_call(
        forward_kernel,
        (piece, piece, piece, piece, kept, kept, square),
        work() + [pltpu.VMEM((edges, ORDERS * LANES), BF16), pltpu.VMEM((edges, LANES), F32)],
        4 * 10**9,
        20 * 10**6,
    )(own_table, partner_table, *far_pieces, src_col, tgt_row, turn, back, radial_basis, weight_radial, *weights)

    agg_pair = collect(aggs)
    own_grad, near_grad, *far_grads, grad_basis = kernel_call(
        backward_kernel,
        (whole, whole, piece, piece, piece, piece, square),
        work()
        + [
            pltpu.VMEM((edges, ORDERS * LANES), F32),
            pltpu.VMEM((edges, ORDERS * LANES), BF16),
            pltpu.VMEM((edges, LANES), F32),
        ],
        5 * 10**9,
        20 * 10**6,
    )(*up_pieces, tgt_col, src_row, turn, back, turned, outs, pre, weight_radial, *weights)

    *far_grads, near_grad, agg_pair = after(*far_grads, near_grad, agg_pair)
    far_home = swap_far(collect(far_grads).astype(BF16)).astype(F32)
    aggregate = agg_pair[:atoms] + across(agg_pair[atoms:].astype(BF16)).astype(F32)
    updated = (
        embeddings.astype(F32) + gain[:, None, :] * scale * aggregate.reshape(embeddings.shape)
    ).astype(BF16)
    summed = own_grad.astype(F32) + swap_near(near_grad).astype(F32)
    parts = [summed[2 * atoms * d : 2 * atoms * (d + 1)].astype(BF16) for d in range(4)]
    grad_pair = collect(parts) + far_home
    grad_rows = grad_pair[:atoms] + across(grad_pair[atoms:].astype(BF16)).astype(F32)
    grad_embeddings = cotangent.astype(F32) + grad_rows.reshape(cotangent.shape)
    return (updated, grad_embeddings, grad_basis)


def solution(mesh):
    both = ("space", "edge")
    placed = (
        P(both, None, None), P(both), P(), P(both), P(both), P("space"), P("space", None),
        P("space", None), P(None, both), P(both, None), P(), P(), P(), P(), P(), P(),
        P(both, None, None),
    )
    return jax.shard_map(
        on_device,
        mesh=mesh,
        in_specs=placed,
        out_specs=(P(both, None, None), P(both, None, None), P(both, None)),
        check_vma=False,
    )
```

```python
import jax
import jax.numpy as jnp
from jax import lax
from jax.experimental import pallas as pl
from jax.experimental.pallas import tpu as pltpu
from jax.sharding import PartitionSpec as P

F32 = jnp.float32
BF16 = jnp.bfloat16
LANES = 128
GROUP = 16
TOP = 6
COEFS = (TOP + 1) ** 2
ORDERS = 29
WIDE = COEFS * LANES
VMEM = 50 * 2**20

TILES = ((0, 1, 2, 3), (4,), (5,), (6,))


def place_of(degree, order):
    if order == 0:
        return degree
    start = {1: 7, -1: 13, 2: 19, -2: 24}[order]
    return start + degree - abs(order)


def tile_table():
    table = []
    row_start = 0
    for degrees in TILES:
        first = degrees[0] ** 2
        coefs = (degrees[-1] + 1) ** 2 - first
        pairs = [(d, m) for d in degrees for m in range(-min(d, 2), min(d, 2) + 1)]
        table.append((first, coefs, pairs, row_start))
        row_start += GROUP * len(pairs)
    return table, row_start


TABLE, TURN_ROWS = tile_table()
BACK_ROWS = GROUP * COEFS
ROT_ROWS = 235
ROT_PAD = 256


def selectors():
    row = lax.broadcasted_iota(jnp.int32, (8, ROT_PAD), 1)
    pair_all, coef_all, pair_tile, coef_tile = [jnp.full(row.shape, -1, jnp.int32) for _ in range(4)]
    offset = 0
    for degree in range(TOP + 1):
        cap, columns = min(degree, 2), 2 * degree + 1
        [(first, _, pairs, start)] = [e for e, d in zip(TABLE, TILES) if degree in d]
        for order in range(-cap, cap + 1):
            place = pairs.index((degree, order))
            inside = (row >= offset) & (row < offset + columns)
            coef = row - offset + degree * degree
            pair_all = jnp.where(inside, start // GROUP + place, pair_all)
            coef_all = jnp.where(inside, coef, coef_all)
            pair_tile = jnp.where(inside, place, pair_tile)
            coef_tile = jnp.where(inside, coef - first, coef_tile)
            offset += columns
    return pair_all[:1], coef_all[:1], pair_tile.astype(F32).T[:, :1], coef_tile.astype(F32).T[:, :1]


def dot(a, b):
    return jnp.dot(a, b, preferred_element_type=F32)


def dot_nt(a, b):
    return lax.dot_general(a, b, (((1,), (1,)), ((), ())), preferred_element_type=F32)


def chunks(total, size):
    return [(s, min(size, total - s)) for s in range(0, total, size)]


def prep_kernel(rot, turn, back, rows_all):
    pair_all, coef_all, pair_tile, coef_tile = selectors()
    rows_all[...] = jnp.zeros_like(rows_all)
    rows_all[pl.ds(0, ROT_ROWS), :] = rot[...]
    row = lax.broadcasted_iota(jnp.int32, (LANES, 256), 0)
    lane = lax.broadcasted_iota(jnp.int32, (LANES, 256), 1) & (GROUP - 1)

    def keep(rows):
        r = lax.broadcasted_iota(jnp.int32, (rows, 256), 0) & (GROUP - 1)
        c = lax.broadcasted_iota(jnp.int32, (rows, 256), 1) & (GROUP - 1)
        return r == c

    def pick(rows, ids):
        group = lax.broadcasted_iota(jnp.int32, (rows, ROT_PAD), 0) // GROUP
        return (group == ids).astype(F32).astype(BF16)

    def mask(ids):
        return lax.broadcasted_iota(jnp.int32, (ROT_PAD, 256), 1) // GROUP == ids.astype(jnp.int32)

    work = (
        (mask(coef_tile), pick(TURN_ROWS, pair_all), keep(TURN_ROWS), turn),
        (mask(pair_tile), pick(BACK_ROWS, coef_all), keep(BACK_ROWS), back),
    )
    for g in range(LANES // GROUP):
        spread = (row == lane + GROUP * g).astype(F32).astype(BF16)
        laid = dot(rows_all[...], spread)
        for masked, picked, kept, out in work:
            full = dot(picked, jnp.where(masked, laid, 0.0).astype(BF16))
            out[g] = jnp.where(kept, full, 0.0).astype(BF16)


def rotate(turn, wide, use):
    for g in range(LANES // GROUP):
        rows = pl.ds(GROUP * g, GROUP)
        for first, coefs, pairs, start in TABLE:
            window = jnp.concatenate(
                [wide[rows, pl.ds((first + c) * LANES, LANES)] for c in range(coefs)], axis=0
            )
            block = turn[g, pl.ds(start, GROUP * len(pairs)), pl.ds(0, GROUP * coefs)]
            result = dot(block, window)
            for k, (degree, order) in enumerate(pairs):
                use(g, degree, order, result[GROUP * k : GROUP * (k + 1)])


def rotate_back(back, fragments, wide):
    for g in range(LANES // GROUP):
        rows = pl.ds(GROUP * g, GROUP)
        for first, coefs, pairs, _ in TABLE:
            window = jnp.concatenate(
                [fragments[rows, pl.ds(place_of(*p) * LANES, LANES)] for p in pairs], axis=0
            )
            block = back[g, pl.ds(GROUP * first, GROUP * coefs), pl.ds(0, GROUP * len(pairs))]
            result = dot(block, window)
            for c in range(coefs):
                wide[rows, pl.ds((first + c) * LANES, LANES)] = result[
                    GROUP * c : GROUP * (c + 1)
                ].astype(BF16)


def pick_rows(ids, pieces, wide):
    total = sum(p.shape[0] for p in pieces)
    hot = (ids[...] == lax.broadcasted_iota(jnp.int32, (LANES, total), 1)).astype(F32).astype(BF16)
    for start, size in chunks(WIDE, 256):
        lanes = pl.ds(start, size)
        table = jnp.concatenate([p[:, lanes] for p in pieces], axis=0)
        wide[:, lanes] = dot(hot, table).astype(BF16)


def add_rows(ids, wide, pieces):
    total = sum(p.shape[0] for p in pieces)
    hot = (ids[...] == lax.broadcasted_iota(jnp.int32, (total, LANES), 0)).astype(F32).astype(BF16)
    for start, size in chunks(WIDE, 256):
        lanes = pl.ds(start, size)
        summed = dot(hot, wide[:, lanes]).astype(BF16)
        offset = 0
        for p in pieces:
            p[:, lanes] = summed[offset : offset + p.shape[0]]
            offset += p.shape[0]


def put_order(zero, one, two, g, degree, order, value):
    where, lead = {0: (zero, 0), 1: (one, 1), 2: (two, 2)}[abs(order)]
    base = LANES if order < 0 else 0
    where[pl.ds(base + GROUP * g, GROUP), pl.ds((degree - lead) * LANES, LANES)] = value


def forward_kernel(
    own, partner, far0, far1, far2, far3, src, tgt, turn, back, basis, w_rad, w0, w1r, w1i, w2r, w2i,
    agg0, agg1, agg2, agg3, turned, outs, pre,
    wide, zero, one, two, gated, rad,
):
    value = dot(basis[...], w_rad[...])
    pre[...] = value
    rad[...] = value * jax.nn.sigmoid(value)
    pick_rows(src, (own, partner, far0, far1, far2, far3), wide)

    def use(g, degree, order, part):
        rows = pl.ds(GROUP * g, GROUP)
        turned[rows, pl.ds(place_of(degree, order) * LANES, LANES)] = part
        put_order(zero, one, two, g, degree, order, (part * rad[rows, :]).astype(BF16))

    rotate(turn, wide, use)
    for start, size in chunks(7 * LANES, 256):
        outs[:, pl.ds(start, size)] = dot(zero[...], w0[:, pl.ds(start, size)])
    for stacked, real, imag, up, down, count in (
        (one, w1r, w1i, 7, 13, 6),
        (two, w2r, w2i, 19, 24, 5),
    ):
        for start, size in chunks(count * LANES, 256):
            a = dot(stacked[...], real[:, pl.ds(start, size)])
            b = dot(stacked[...], imag[:, pl.ds(start, size)])
            outs[:, pl.ds(up * LANES + start, size)] = a[:LANES] - b[LANES:]
            outs[:, pl.ds(down * LANES + start, size)] = a[LANES:] + b[:LANES]
    gate = jax.nn.sigmoid(outs[:, pl.ds(0, LANES)])
    for q in range(ORDERS):
        lanes = pl.ds(q * LANES, LANES)
        gated[:, lanes] = (outs[:, lanes] * gate).astype(BF16)
    rotate_back(back, gated, wide)
    add_rows(tgt, wide, (agg0, agg1, agg2, agg3))


def backward_kernel(
    up0, up1, up2, up3, tgt, src, turn, back, turned, outs, pre, w_rad, w0, w1r, w1i, w2r, w2i,
    own, partner, far0, far1, far2, far3, grad_basis,
    wide, zero, one, two, grads, fragments, rad,
):
    pick_rows(tgt, (up0, up1, up2, up3), wide)

    def use(g, degree, order, part):
        grads[pl.ds(GROUP * g, GROUP), pl.ds(place_of(degree, order) * LANES, LANES)] = part

    rotate(turn, wide, use)
    scalar = outs[:, pl.ds(0, LANES)]
    gate = jax.nn.sigmoid(scalar)
    slope = gate * (1.0 - gate)
    lead = grads[:, pl.ds(0, LANES)]
    weighted = lead * scalar
    for q in range(1, ORDERS):
        lanes = pl.ds(q * LANES, LANES)
        weighted = weighted + grads[:, lanes] * outs[:, lanes]
    zero[:, pl.ds(0, LANES)] = (
        lead * (gate + scalar * slope) + slope * (weighted - lead * scalar)
    ).astype(BF16)
    for stacked, count, base, q0 in ((zero, 6, 0, 1), (one, 6, 0, 7), (one, 6, LANES, 13), (two, 5, 0, 19), (two, 5, LANES, 24)):
        for k in range(count):
            value = (grads[:, pl.ds((q0 + k) * LANES, LANES)] * gate).astype(BF16)
            column = k + 1 if stacked is zero else k
            stacked[pl.ds(base, LANES), pl.ds(column * LANES, LANES)] = value
    value = pre[...]
    gate = jax.nn.sigmoid(value)
    rad[...] = value * gate
    slope = gate * (1.0 + value * (1.0 - gate))
    total = jnp.zeros((LANES, LANES), F32)

    def take(total, q, scaled):
        lanes = pl.ds(q * LANES, LANES)
        fragments[:, lanes] = (scaled * rad[...]).astype(BF16)
        return total + scaled * turned[:, lanes]

    for start, size in chunks(7 * LANES, 256):
        a = dot_nt(zero[...], w0[pl.ds(start, size), :])
        for k in range(size // LANES):
            total = take(total, start // LANES + k, a[:, k * LANES : (k + 1) * LANES])
    for stacked, real, imag, up, down, count in (
        (one, w1r, w1i, 7, 13, 6),
        (two, w2r, w2i, 19, 24, 5),
    ):
        for start, size in chunks(count * LANES, 256):
            a = dot_nt(stacked[...], real[pl.ds(start, size), :])
            b = dot_nt(stacked[...], imag[pl.ds(start, size), :])
            for k in range(size // LANES):
                cut = slice(k * LANES, (k + 1) * LANES)
                total = take(total, up + start // LANES + k, a[:LANES, cut] + b[LANES:, cut])
                total = take(total, down + start // LANES + k, a[LANES:, cut] - b[:LANES, cut])
    grad_basis[...] = dot_nt((total * slope).astype(BF16), w_rad[...])
    rotate_back(back, fragments, wide)
    add_rows(src, wide, (own, partner, far0, far1, far2, far3))


def kernel_call(kernel, outs, scratch, flops, moved):
    return pl.pallas_call(
        kernel,
        out_shape=outs,
        scratch_shapes=scratch,
        compiler_params=pltpu.CompilerParams(vmem_limit_bytes=VMEM),
        cost_estimate=pl.CostEstimate(flops=flops, bytes_accessed=moved, transcendentals=0),
    )


def shaped(*dims, kind=BF16):
    return jax.ShapeDtypeStruct(dims, kind)


def on_device(
    embeddings, species, species_gain, sources, targets, counts, send_left, send_right, rotations,
    radial_basis, weight_radial, weight_zero, weight_one_real, weight_one_imag, weight_two_real,
    weight_two_imag, cotangent,
):
    weights = (weight_zero, weight_one_real, weight_one_imag, weight_two_real, weight_two_imag)
    atoms = embeddings.shape[0]
    edges = sources.shape[0]
    blocks = lax.axis_size("space")
    member = lax.axis_index("edge")
    block = lax.axis_index("space")
    half, along = member // 4, member % 4
    odd = block % 2
    scale = (atoms / edges) ** 0.5

    def across(v):
        return lax.ppermute(v, "edge", [(s, (s + 4) % 8) for s in range(8)])

    def shift(v, k):
        return lax.ppermute(v, "edge", [(s, s // 4 * 4 + (s + k) % 4) for s in range(8)])

    def swap_near(v):
        return lax.ppermute(v, "space", [(b, b ^ 1) for b in range(blocks)])

    def swap_far(v):
        return lax.ppermute(v, "space", [(b, (b + 2 * (b % 2) - 1) % blocks) for b in range(blocks)])

    def roll(v, k):
        return lax.ppermute(v, "space", [(b, (b + k) % blocks) for b in range(blocks)])

    def after(*values):
        return lax.optimization_barrier(values)

    def spread(v):
        return [v] + [shift(v, 4 - d) for d in (1, 2, 3)]

    def collect(parts):
        total = parts[0].astype(F32)
        for d in (1, 2, 3):
            total = total + shift(parts[d], d).astype(F32)
        return total

    groups = LANES // GROUP
    turn, back = kernel_call(
        prep_kernel,
        (shaped(groups, TURN_ROWS, 256), shaped(groups, BACK_ROWS, 256)),
        [pltpu.VMEM((ROT_PAD, LANES), BF16)],
        2 * 10**9,
        6 * 10**6,
    )(rotations)

    flat = embeddings.reshape(atoms, WIDE)
    beyond, back = after(across(flat), back)
    pair = jnp.concatenate([flat, beyond], axis=0)
    pair, species, cot, targets = after(pair, species, cotangent, targets)
    far_pair = swap_far(pair)
    own_pieces = spread(pair)
    gain = jnp.dot(
        (species[:, None] == lax.iota(jnp.int32, species_gain.shape[0])[None, :]).astype(F32),
        species_gain,
        precision=lax.Precision.HIGHEST,
    )
    upstream = (cot.astype(F32) * gain[:, None, :] * scale).astype(BF16).reshape(atoms, WIDE)
    far_pair, upstream, send_left, send_right, sources = after(
        far_pair, upstream, send_left, send_right, sources
    )
    far_pieces = spread(far_pair)
    own_table = jnp.concatenate(own_pieces, axis=0)
    partner_table = swap_near(own_table)
    *far_pieces, up_far = after(*far_pieces, across(upstream))
    up_pair = jnp.concatenate([upstream, up_far], axis=0)
    up_pieces = spread(up_pair)

    def slot(atom):
        owner, row = atom // atoms, atom % atoms
        return (owner % 4 - along) % 4 * (2 * atoms) + (owner // 4 - half) % 2 * atoms + row

    lists = jnp.concatenate([roll(send_right, 1), roll(send_left, -1)], axis=1)[0]
    halo = send_left.shape[1]
    block_atoms = 8 * atoms
    halo_hot = (sources[:, None] - block_atoms) == lax.iota(jnp.int32, 2 * halo)[None, :]
    halo_atom = jnp.sum(jnp.where(halo_hot, lists[None, :], 0), axis=1)
    on_left = sources < block_atoms + halo
    near = jnp.where(on_left, odd == 1, odd == 0)
    src = jnp.where(
        sources < block_atoms,
        slot(sources),
        jnp.where(near, block_atoms, 2 * block_atoms) + slot(halo_atom),
    ).astype(jnp.int32)
    live = member * edges + lax.iota(jnp.int32, edges) < counts[0]
    tgt = jnp.where(live, slot(targets), -1).astype(jnp.int32)
    src_col, src_row = src[:, None], src[None, :]
    tgt_col, tgt_row = tgt[:, None], tgt[None, :]

    def work():
        return [
            pltpu.VMEM((edges, WIDE), BF16),
            pltpu.VMEM((edges, 7 * LANES), BF16),
            pltpu.VMEM((2 * edges, 6 * LANES), BF16),
            pltpu.VMEM((2 * edges, 5 * LANES), BF16),
        ]

    piece = shaped(2 * atoms, WIDE)
    whole = shaped(block_atoms, WIDE)
    kept = shaped(edges, ORDERS * LANES, kind=F32)
    square = shaped(edges, LANES, kind=F32)
    *aggs, turned, outs, pre = kernel_call(
        forward_kernel,
        (piece, piece, piece, piece, kept, kept, square),
        work() + [pltpu.VMEM((edges, ORDERS * LANES), BF16), pltpu.VMEM((edges, LANES), F32)],
        4 * 10**9,
        20 * 10**6,
    )(own_table, partner_table, *far_pieces, src_col, tgt_row, turn, back, radial_basis, weight_radial, *weights)

    agg_pair = collect(aggs)
    own_grad, near_grad, *far_grads, grad_basis = kernel_call(
        backward_kernel,
        (whole, whole, piece, piece, piece, piece, square),
        work()
        + [
            pltpu.VMEM((edges, ORDERS * LANES), F32),
            pltpu.VMEM((edges, ORDERS * LANES), BF16),
            pltpu.VMEM((edges, LANES), F32),
        ],
        5 * 10**9,
        20 * 10**6,
    )(*up_pieces, tgt_col, src_row, turn, back, turned, outs, pre, weight_radial, *weights)

    *far_grads, near_grad, agg_pair = after(*far_grads, near_grad, agg_pair)
    near_home, agg_far = after(swap_near(near_grad), across(agg_pair[atoms:].astype(BF16)))
    far_home = swap_far(collect(far_grads).astype(BF16)).astype(F32)
    aggregate = agg_pair[:atoms] + agg_far.astype(F32)
    updated = (
        embeddings.astype(F32) + gain[:, None, :] * scale * aggregate.reshape(embeddings.shape)
    ).astype(BF16)
    summed = own_grad.astype(F32) + near_home.astype(F32)
    parts = [summed[2 * atoms * d : 2 * atoms * (d + 1)].astype(BF16) for d in range(4)]
    grad_pair = collect(parts) + far_home
    grad_rows = grad_pair[:atoms] + across(grad_pair[atoms:].astype(BF16)).astype(F32)
    grad_embeddings = cotangent.astype(F32) + grad_rows.reshape(cotangent.shape)
    return (updated, grad_embeddings, grad_basis)


def solution(mesh):
    both = ("space", "edge")
    placed = (
        P(both, None, None), P(both), P(), P(both), P(both), P("space"), P("space", None),
        P("space", None), P(None, both), P(both, None), P(), P(), P(), P(), P(), P(),
        P(both, None, None),
    )
    return jax.shard_map(
        on_device,
        mesh=mesh,
        in_specs=placed,
        out_specs=(P(both, None, None), P(both, None, None), P(both, None)),
        check_vma=False,
    )
```

```python
import jax
import jax.numpy as jnp
from jax import lax
from jax.experimental import pallas as pl
from jax.experimental.pallas import tpu as pltpu
from jax.sharding import PartitionSpec as P

F32 = jnp.float32
BF16 = jnp.bfloat16
LANES = 128
GROUP = 16
TOP = 6
COEFS = (TOP + 1) ** 2
ORDERS = 29
WIDE = COEFS * LANES
VMEM = 50 * 2**20

TILES = ((0, 1, 2, 3), (4,), (5,), (6,))


def place_of(degree, order):
    if order == 0:
        return degree
    start = {1: 7, -1: 13, 2: 19, -2: 24}[order]
    return start + degree - abs(order)


def tile_table():
    table = []
    row_start = 0
    for degrees in TILES:
        first = degrees[0] ** 2
        coefs = (degrees[-1] + 1) ** 2 - first
        pairs = [(d, m) for d in degrees for m in range(-min(d, 2), min(d, 2) + 1)]
        table.append((first, coefs, pairs, row_start))
        row_start += GROUP * len(pairs)
    return table, row_start


TABLE, TURN_ROWS = tile_table()
BACK_ROWS = GROUP * COEFS
ROT_ROWS = 235
ROT_PAD = 256


def selectors():
    row = lax.broadcasted_iota(jnp.int32, (8, ROT_PAD), 1)
    pair_all, coef_all, pair_tile, coef_tile = [jnp.full(row.shape, -1, jnp.int32) for _ in range(4)]
    offset = 0
    for degree in range(TOP + 1):
        cap, columns = min(degree, 2), 2 * degree + 1
        [(first, _, pairs, start)] = [e for e, d in zip(TABLE, TILES) if degree in d]
        for order in range(-cap, cap + 1):
            place = pairs.index((degree, order))
            inside = (row >= offset) & (row < offset + columns)
            coef = row - offset + degree * degree
            pair_all = jnp.where(inside, start // GROUP + place, pair_all)
            coef_all = jnp.where(inside, coef, coef_all)
            pair_tile = jnp.where(inside, place, pair_tile)
            coef_tile = jnp.where(inside, coef - first, coef_tile)
            offset += columns
    return pair_all[:1], coef_all[:1], pair_tile.astype(F32).T[:, :1], coef_tile.astype(F32).T[:, :1]


def dot(a, b):
    return jnp.dot(a, b, preferred_element_type=F32)


def dot_nt(a, b):
    return lax.dot_general(a, b, (((1,), (1,)), ((), ())), preferred_element_type=F32)


def chunks(total, size):
    return [(s, min(size, total - s)) for s in range(0, total, size)]


def copies(sources, places, sems, first):
    return [
        pltpu.make_async_copy(a, b, sems.at[first + k]) for k, (a, b) in enumerate(zip(sources, places))
    ]


def prep_kernel(rot, turn, back, rows_all):
    pair_all, coef_all, pair_tile, coef_tile = selectors()
    rows_all[...] = jnp.zeros_like(rows_all)
    rows_all[pl.ds(0, ROT_ROWS), :] = rot[...]
    row = lax.broadcasted_iota(jnp.int32, (LANES, 256), 0)
    lane = lax.broadcasted_iota(jnp.int32, (LANES, 256), 1) & (GROUP - 1)

    def keep(rows):
        r = lax.broadcasted_iota(jnp.int32, (rows, 256), 0) & (GROUP - 1)
        c = lax.broadcasted_iota(jnp.int32, (rows, 256), 1) & (GROUP - 1)
        return r == c

    def pick(rows, ids):
        group = lax.broadcasted_iota(jnp.int32, (rows, ROT_PAD), 0) // GROUP
        return (group == ids).astype(F32).astype(BF16)

    def mask(ids):
        return lax.broadcasted_iota(jnp.int32, (ROT_PAD, 256), 1) // GROUP == ids.astype(jnp.int32)

    work = (
        (mask(coef_tile), pick(TURN_ROWS, pair_all), keep(TURN_ROWS), turn),
        (mask(pair_tile), pick(BACK_ROWS, coef_all), keep(BACK_ROWS), back),
    )
    for g in range(LANES // GROUP):
        spread = (row == lane + GROUP * g).astype(F32).astype(BF16)
        laid = dot(rows_all[...], spread)
        for masked, picked, kept, out in work:
            full = dot(picked, jnp.where(masked, laid, 0.0).astype(BF16))
            out[g] = jnp.where(kept, full, 0.0).astype(BF16)


def rotate(turn, wide, use):
    for g in range(LANES // GROUP):
        rows = pl.ds(GROUP * g, GROUP)
        for first, coefs, pairs, start in TABLE:
            window = jnp.concatenate(
                [wide[rows, pl.ds((first + c) * LANES, LANES)] for c in range(coefs)], axis=0
            )
            block = turn[g, pl.ds(start, GROUP * len(pairs)), pl.ds(0, GROUP * coefs)]
            result = dot(block, window)
            for k, (degree, order) in enumerate(pairs):
                use(g, degree, order, result[GROUP * k : GROUP * (k + 1)])


def rotate_back(back, fragments, wide):
    for g in range(LANES // GROUP):
        rows = pl.ds(GROUP * g, GROUP)
        for first, coefs, pairs, _ in TABLE:
            window = jnp.concatenate(
                [fragments[rows, pl.ds(place_of(*p) * LANES, LANES)] for p in pairs], axis=0
            )
            block = back[g, pl.ds(GROUP * first, GROUP * coefs), pl.ds(0, GROUP * len(pairs))]
            result = dot(block, window)
            for c in range(coefs):
                wide[rows, pl.ds((first + c) * LANES, LANES)] = result[
                    GROUP * c : GROUP * (c + 1)
                ].astype(BF16)


def pick_rows(ids, pieces, wide):
    total = sum(p.shape[0] for p in pieces)
    hot = (ids[...] == lax.broadcasted_iota(jnp.int32, (LANES, total), 1)).astype(F32).astype(BF16)
    for start, size in chunks(WIDE, 256):
        lanes = pl.ds(start, size)
        table = jnp.concatenate([p[:, lanes] for p in pieces], axis=0)
        wide[:, lanes] = dot(hot, table).astype(BF16)


def add_rows(ids, wide, pieces):
    total = sum(p.shape[0] for p in pieces)
    hot = (ids[...] == lax.broadcasted_iota(jnp.int32, (total, LANES), 0)).astype(F32).astype(BF16)
    for start, size in chunks(WIDE, 256):
        lanes = pl.ds(start, size)
        summed = dot(hot, wide[:, lanes]).astype(BF16)
        offset = 0
        for p in pieces:
            p[:, lanes] = summed[offset : offset + p.shape[0]]
            offset += p.shape[0]


def put_order(zero, one, two, g, degree, order, value):
    where, lead = {0: (zero, 0), 1: (one, 1), 2: (two, 2)}[abs(order)]
    base = LANES if order < 0 else 0
    where[pl.ds(base + GROUP * g, GROUP), pl.ds((degree - lead) * LANES, LANES)] = value


def forward_kernel(
    own, partner, far0, far1, far2, far3, src, tgt, turn, basis, w_rad,
    w0_far, w1r_far, w1i_far, w2r_far, w2i_far, back_far,
    agg0, agg1, agg2, agg3, pre, turned_far, outs_far,
    wide, zero, one, two, w0, w1r, w1i, w2r, w2i, back, turned, outs, gated, rad, sems,
):
    loads = copies(
        (w0_far, w1r_far, w1i_far, w2r_far, w2i_far, back_far), (w0, w1r, w1i, w2r, w2i, back), sems, 0
    )
    stores = copies((turned, outs), (turned_far, outs_far), sems, 6)
    for c in loads:
        c.start()
    value = dot(basis[...], w_rad[...])
    pre[...] = value
    rad[...] = value * jax.nn.sigmoid(value)
    pick_rows(src, (own, partner, far0, far1, far2, far3), wide)

    def use(g, degree, order, part):
        rows = pl.ds(GROUP * g, GROUP)
        turned[rows, pl.ds(place_of(degree, order) * LANES, LANES)] = part
        put_order(zero, one, two, g, degree, order, (part * rad[rows, :]).astype(BF16))

    rotate(turn, wide, use)
    stores[0].start()
    for c in loads[:5]:
        c.wait()
    for start, size in chunks(7 * LANES, 256):
        outs[:, pl.ds(start, size)] = dot(zero[...], w0[:, pl.ds(start, size)])
    for stacked, real, imag, up, down, count in (
        (one, w1r, w1i, 7, 13, 6),
        (two, w2r, w2i, 19, 24, 5),
    ):
        for start, size in chunks(count * LANES, 256):
            a = dot(stacked[...], real[:, pl.ds(start, size)])
            b = dot(stacked[...], imag[:, pl.ds(start, size)])
            outs[:, pl.ds(up * LANES + start, size)] = a[:LANES] - b[LANES:]
            outs[:, pl.ds(down * LANES + start, size)] = a[LANES:] + b[:LANES]
    stores[1].start()
    gate = jax.nn.sigmoid(outs[:, pl.ds(0, LANES)])
    for q in range(ORDERS):
        lanes = pl.ds(q * LANES, LANES)
        gated[:, lanes] = (outs[:, lanes] * gate).astype(BF16)
    loads[5].wait()
    rotate_back(back, gated, wide)
    add_rows(tgt, wide, (agg0, agg1, agg2, agg3))
    for c in stores:
        c.wait()


def backward_kernel(
    up0, up1, up2, up3, tgt, src, turn, pre, w_rad,
    outs_far, w0_far, w1r_far, w1i_far, w2r_far, w2i_far, turned_far, back_far,
    own, partner, far0, far1, far2, far3, grad_basis,
    wide, zero, one, two, w0, w1r, w1i, w2r, w2i, back, turned, outs, grads, fragments, rad, sems,
):
    loads = copies(
        (outs_far, w0_far, w1r_far, w1i_far, w2r_far, w2i_far, turned_far, back_far),
        (outs, w0, w1r, w1i, w2r, w2i, turned, back),
        sems,
        0,
    )
    for c in loads:
        c.start()
    pick_rows(tgt, (up0, up1, up2, up3), wide)

    def use(g, degree, order, part):
        grads[pl.ds(GROUP * g, GROUP), pl.ds(place_of(degree, order) * LANES, LANES)] = part

    rotate(turn, wide, use)
    loads[0].wait()
    scalar = outs[:, pl.ds(0, LANES)]
    gate = jax.nn.sigmoid(scalar)
    slope = gate * (1.0 - gate)
    lead = grads[:, pl.ds(0, LANES)]
    weighted = lead * scalar
    for q in range(1, ORDERS):
        lanes = pl.ds(q * LANES, LANES)
        weighted = weighted + grads[:, lanes] * outs[:, lanes]
    zero[:, pl.ds(0, LANES)] = (
        lead * (gate + scalar * slope) + slope * (weighted - lead * scalar)
    ).astype(BF16)
    for stacked, count, base, q0 in ((zero, 6, 0, 1), (one, 6, 0, 7), (one, 6, LANES, 13), (two, 5, 0, 19), (two, 5, LANES, 24)):
        for k in range(count):
            value = (grads[:, pl.ds((q0 + k) * LANES, LANES)] * gate).astype(BF16)
            column = k + 1 if stacked is zero else k
            stacked[pl.ds(base, LANES), pl.ds(column * LANES, LANES)] = value
    value = pre[...]
    gate = jax.nn.sigmoid(value)
    rad[...] = value * gate
    slope = gate * (1.0 + value * (1.0 - gate))
    total = jnp.zeros((LANES, LANES), F32)

    def take(total, q, scaled):
        lanes = pl.ds(q * LANES, LANES)
        fragments[:, lanes] = (scaled * rad[...]).astype(BF16)
        return total + scaled * turned[:, lanes]

    for c in loads[1:7]:
        c.wait()
    for start, size in chunks(7 * LANES, 256):
        a = dot_nt(zero[...], w0[pl.ds(start, size), :])
        for k in range(size // LANES):
            total = take(total, start // LANES + k, a[:, k * LANES : (k + 1) * LANES])
    for stacked, real, imag, up, down, count in (
        (one, w1r, w1i, 7, 13, 6),
        (two, w2r, w2i, 19, 24, 5),
    ):
        for start, size in chunks(count * LANES, 256):
            a = dot_nt(stacked[...], real[pl.ds(start, size), :])
            b = dot_nt(stacked[...], imag[pl.ds(start, size), :])
            for k in range(size // LANES):
                cut = slice(k * LANES, (k + 1) * LANES)
                total = take(total, up + start // LANES + k, a[:LANES, cut] + b[LANES:, cut])
                total = take(total, down + start // LANES + k, a[LANES:, cut] - b[:LANES, cut])
    grad_basis[...] = dot_nt((total * slope).astype(BF16), w_rad[...])
    loads[7].wait()
    rotate_back(back, fragments, wide)
    add_rows(src, wide, (own, partner, far0, far1, far2, far3))


def kernel_call(kernel, near, far, outs, far_outs, scratch, flops, moved):
    inside, outside = pl.BlockSpec(memory_space=pltpu.VMEM), pl.BlockSpec(memory_space=pl.ANY)
    return pl.pallas_call(
        kernel,
        out_shape=outs + far_outs,
        in_specs=[inside] * near + [outside] * far,
        out_specs=(inside,) * len(outs) + (outside,) * len(far_outs),
        scratch_shapes=scratch,
        compiler_params=pltpu.CompilerParams(vmem_limit_bytes=VMEM),
        cost_estimate=pl.CostEstimate(flops=flops, bytes_accessed=moved, transcendentals=0),
    )


def shaped(*dims, kind=BF16):
    return jax.ShapeDtypeStruct(dims, kind)


def on_device(
    embeddings, species, species_gain, sources, targets, counts, send_left, send_right, rotations,
    radial_basis, weight_radial, weight_zero, weight_one_real, weight_one_imag, weight_two_real,
    weight_two_imag, cotangent,
):
    weights = (weight_zero, weight_one_real, weight_one_imag, weight_two_real, weight_two_imag)
    atoms = embeddings.shape[0]
    edges = sources.shape[0]
    blocks = lax.axis_size("space")
    member = lax.axis_index("edge")
    block = lax.axis_index("space")
    half, along = member // 4, member % 4
    odd = block % 2
    scale = (atoms / edges) ** 0.5

    def across(v):
        return lax.ppermute(v, "edge", [(s, (s + 4) % 8) for s in range(8)])

    def shift(v, k):
        return lax.ppermute(v, "edge", [(s, s // 4 * 4 + (s + k) % 4) for s in range(8)])

    def swap_near(v):
        return lax.ppermute(v, "space", [(b, b ^ 1) for b in range(blocks)])

    def swap_far(v):
        return lax.ppermute(v, "space", [(b, (b + 2 * (b % 2) - 1) % blocks) for b in range(blocks)])

    def roll(v, k):
        return lax.ppermute(v, "space", [(b, (b + k) % blocks) for b in range(blocks)])

    def after(*values):
        return lax.optimization_barrier(values)

    def spread(v):
        return [v] + [shift(v, 4 - d) for d in (1, 2, 3)]

    def collect(parts):
        total = parts[0].astype(F32)
        for d in (1, 2, 3):
            total = total + shift(parts[d], d).astype(F32)
        return total

    flat = embeddings.reshape(atoms, WIDE)
    pair = jnp.concatenate([flat, across(flat)], axis=0)
    gain = jnp.dot(
        (species[:, None] == lax.iota(jnp.int32, species_gain.shape[0])[None, :]).astype(F32),
        species_gain,
        precision=lax.Precision.HIGHEST,
    )
    upstream = (cotangent.astype(F32) * gain[:, None, :] * scale).astype(BF16).reshape(atoms, WIDE)
    up_far = across(upstream)
    pair, rotations, targets = after(pair, rotations, targets)
    far_pair = swap_far(pair)
    own_pieces = spread(pair)
    groups = LANES // GROUP
    turn, back = kernel_call(
        prep_kernel,
        1,
        0,
        (shaped(groups, TURN_ROWS, 256), shaped(groups, BACK_ROWS, 256)),
        (),
        [pltpu.VMEM((ROT_PAD, LANES), BF16)],
        2 * 10**9,
        6 * 10**6,
    )(rotations)

    far_pair, back, send_left, send_right, sources = after(
        far_pair, back, send_left, send_right, sources
    )
    *own_pieces, back = after(*own_pieces, back)
    far_pieces = spread(far_pair)
    own_table = jnp.concatenate(own_pieces, axis=0)
    partner_table = swap_near(own_table)
    *far_pieces, up_far = after(*far_pieces, up_far)
    up_pair = jnp.concatenate([upstream, up_far], axis=0)
    up_pieces = spread(up_pair)

    def slot(atom):
        owner, row = atom // atoms, atom % atoms
        return (owner % 4 - along) % 4 * (2 * atoms) + (owner // 4 - half) % 2 * atoms + row

    lists = jnp.concatenate([roll(send_right, 1), roll(send_left, -1)], axis=1)[0]
    halo = send_left.shape[1]
    block_atoms = 8 * atoms
    halo_hot = (sources[:, None] - block_atoms) == lax.iota(jnp.int32, 2 * halo)[None, :]
    halo_atom = jnp.sum(jnp.where(halo_hot, lists[None, :], 0), axis=1)
    on_left = sources < block_atoms + halo
    near = jnp.where(on_left, odd == 1, odd == 0)
    src = jnp.where(
        sources < block_atoms,
        slot(sources),
        jnp.where(near, block_atoms, 2 * block_atoms) + slot(halo_atom),
    ).astype(jnp.int32)
    live = member * edges + lax.iota(jnp.int32, edges) < counts[0]
    tgt = jnp.where(live, slot(targets), -1).astype(jnp.int32)
    src_col, src_row = src[:, None], src[None, :]
    tgt_col, tgt_row = tgt[:, None], tgt[None, :]

    def work():
        return [
            pltpu.VMEM((edges, WIDE), BF16),
            pltpu.VMEM((edges, 7 * LANES), BF16),
            pltpu.VMEM((2 * edges, 6 * LANES), BF16),
            pltpu.VMEM((2 * edges, 5 * LANES), BF16),
            *[pltpu.VMEM(w.shape, BF16) for w in weights],
            pltpu.VMEM(back.shape, BF16),
            pltpu.VMEM((edges, ORDERS * LANES), F32),
            pltpu.VMEM((edges, ORDERS * LANES), F32),
        ]

    piece = shaped(2 * atoms, WIDE)
    whole = shaped(block_atoms, WIDE)
    kept = shaped(edges, ORDERS * LANES, kind=F32)
    square = shaped(edges, LANES, kind=F32)
    *aggs, pre, turned, outs = kernel_call(
        forward_kernel,
        11,
        6,
        (piece, piece, piece, piece, square),
        (kept, kept),
        work()
        + [
            pltpu.VMEM((edges, ORDERS * LANES), BF16),
            pltpu.VMEM((edges, LANES), F32),
            pltpu.SemaphoreType.DMA((8,)),
        ],
        4 * 10**9,
        20 * 10**6,
    )(
        own_table, partner_table, *far_pieces, src_col, tgt_row, turn, radial_basis, weight_radial,
        *weights, back,
    )

    agg_pair = collect(aggs)
    own_grad, near_grad, *far_grads, grad_basis = kernel_call(
        backward_kernel,
        9,
        8,
        (whole, whole, piece, piece, piece, piece, square),
        (),
        work()
        + [
            pltpu.VMEM((edges, ORDERS * LANES), F32),
            pltpu.VMEM((edges, ORDERS * LANES), BF16),
            pltpu.VMEM((edges, LANES), F32),
            pltpu.SemaphoreType.DMA((8,)),
        ],
        5 * 10**9,
        20 * 10**6,
    )(*up_pieces, tgt_col, src_row, turn, pre, weight_radial, outs, *weights, turned, back)

    *far_grads, near_grad, agg_pair = after(*far_grads, near_grad, agg_pair)
    near_home, agg_far = after(swap_near(near_grad), across(agg_pair[atoms:].astype(BF16)))
    far_home = swap_far(collect(far_grads).astype(BF16)).astype(F32)
    aggregate = agg_pair[:atoms] + agg_far.astype(F32)
    updated = (
        embeddings.astype(F32) + gain[:, None, :] * scale * aggregate.reshape(embeddings.shape)
    ).astype(BF16)
    summed = own_grad.astype(F32) + near_home.astype(F32)
    parts = [summed[2 * atoms * d : 2 * atoms * (d + 1)].astype(BF16) for d in range(4)]
    grad_pair = collect(parts) + far_home
    grad_rows = grad_pair[:atoms] + across(grad_pair[atoms:].astype(BF16)).astype(F32)
    grad_embeddings = cotangent.astype(F32) + grad_rows.reshape(cotangent.shape)
    return (updated, grad_embeddings, grad_basis)


def solution(mesh):
    both = ("space", "edge")
    placed = (
        P(both, None, None), P(both), P(), P(both), P(both), P("space"), P("space", None),
        P("space", None), P(None, both), P(both, None), P(), P(), P(), P(), P(), P(),
        P(both, None, None),
    )
    return jax.shard_map(
        on_device,
        mesh=mesh,
        in_specs=placed,
        out_specs=(P(both, None, None), P(both, None, None), P(both, None)),
        check_vma=False,
    )
```

```python
import jax
import jax.numpy as jnp
from jax import lax
from jax.experimental import pallas as pl
from jax.experimental.pallas import tpu as pltpu
from jax.sharding import PartitionSpec as P

F32 = jnp.float32
BF16 = jnp.bfloat16
LANES = 128
GROUP = 16
TOP = 6
COEFS = (TOP + 1) ** 2
ORDERS = 29
WIDE = COEFS * LANES
VMEM = 50 * 2**20

TILES = ((0, 1, 2, 3), (4,), (5,), (6,))


def place_of(degree, order):
    if order == 0:
        return degree
    start = {1: 7, -1: 13, 2: 19, -2: 24}[order]
    return start + degree - abs(order)


def tile_table():
    table = []
    row_start = 0
    for degrees in TILES:
        first = degrees[0] ** 2
        coefs = (degrees[-1] + 1) ** 2 - first
        pairs = [(d, m) for d in degrees for m in range(-min(d, 2), min(d, 2) + 1)]
        table.append((first, coefs, pairs, row_start))
        row_start += GROUP * len(pairs)
    return table, row_start


TABLE, TURN_ROWS = tile_table()
BACK_ROWS = GROUP * COEFS
ROT_ROWS = 235
ROT_PAD = 256


def selectors():
    row = lax.broadcasted_iota(jnp.int32, (8, ROT_PAD), 1)
    pair_all, coef_all, pair_tile, coef_tile = [jnp.full(row.shape, -1, jnp.int32) for _ in range(4)]
    offset = 0
    for degree in range(TOP + 1):
        cap, columns = min(degree, 2), 2 * degree + 1
        [(first, _, pairs, start)] = [e for e, d in zip(TABLE, TILES) if degree in d]
        for order in range(-cap, cap + 1):
            place = pairs.index((degree, order))
            inside = (row >= offset) & (row < offset + columns)
            coef = row - offset + degree * degree
            pair_all = jnp.where(inside, start // GROUP + place, pair_all)
            coef_all = jnp.where(inside, coef, coef_all)
            pair_tile = jnp.where(inside, place, pair_tile)
            coef_tile = jnp.where(inside, coef - first, coef_tile)
            offset += columns
    return pair_all[:1], coef_all[:1], pair_tile.astype(F32).T[:, :1], coef_tile.astype(F32).T[:, :1]


def dot(a, b):
    return jnp.dot(a, b, preferred_element_type=F32)


def dot_nt(a, b):
    return lax.dot_general(a, b, (((1,), (1,)), ((), ())), preferred_element_type=F32)


def chunks(total, size):
    return [(s, min(size, total - s)) for s in range(0, total, size)]


def copies(sources, places, sems, first):
    return [
        pltpu.make_async_copy(a, b, sems.at[first + k]) for k, (a, b) in enumerate(zip(sources, places))
    ]


def prep_kernel(rot, first, turn, back, rows_all):
    pair_all, coef_all, pair_tile, coef_tile = selectors()
    rows_all[...] = jnp.zeros_like(rows_all)
    rows_all[pl.ds(0, ROT_ROWS), :] = rot[...]
    row = lax.broadcasted_iota(jnp.int32, (LANES, 256), 0)
    lane = lax.broadcasted_iota(jnp.int32, (LANES, 256), 1) & (GROUP - 1)

    def keep(rows):
        r = lax.broadcasted_iota(jnp.int32, (rows, 256), 0) & (GROUP - 1)
        c = lax.broadcasted_iota(jnp.int32, (rows, 256), 1) & (GROUP - 1)
        return r == c

    def pick(rows, ids):
        group = lax.broadcasted_iota(jnp.int32, (rows, ROT_PAD), 0) // GROUP
        return (group == ids).astype(F32).astype(BF16)

    def mask(ids):
        return lax.broadcasted_iota(jnp.int32, (ROT_PAD, 256), 1) // GROUP == ids.astype(jnp.int32)

    work = (
        (mask(coef_tile), pick(TURN_ROWS, pair_all), keep(TURN_ROWS), turn),
        (mask(pair_tile), pick(BACK_ROWS, coef_all), keep(BACK_ROWS), back),
    )
    for g in range(LANES // GROUP):
        spread = (row == lane + GROUP * g).astype(F32).astype(BF16)
        laid = dot(rows_all[...], spread)
        for masked, picked, kept, out in work:
            full = dot(picked, jnp.where(masked, laid, 0.0).astype(BF16))
            out[g] = jnp.where(kept, full, 0.0).astype(BF16)


def rotate(turn, wide, use):
    for g in range(LANES // GROUP):
        rows = pl.ds(GROUP * g, GROUP)
        for first, coefs, pairs, start in TABLE:
            window = jnp.concatenate(
                [wide[rows, pl.ds((first + c) * LANES, LANES)] for c in range(coefs)], axis=0
            )
            block = turn[g, pl.ds(start, GROUP * len(pairs)), pl.ds(0, GROUP * coefs)]
            result = dot(block, window)
            for k, (degree, order) in enumerate(pairs):
                use(g, degree, order, result[GROUP * k : GROUP * (k + 1)])


def rotate_back(back, fragments, wide):
    for g in range(LANES // GROUP):
        rows = pl.ds(GROUP * g, GROUP)
        for first, coefs, pairs, _ in TABLE:
            window = jnp.concatenate(
                [fragments[rows, pl.ds(place_of(*p) * LANES, LANES)] for p in pairs], axis=0
            )
            block = back[g, pl.ds(GROUP * first, GROUP * coefs), pl.ds(0, GROUP * len(pairs))]
            result = dot(block, window)
            for c in range(coefs):
                wide[rows, pl.ds((first + c) * LANES, LANES)] = result[
                    GROUP * c : GROUP * (c + 1)
                ].astype(BF16)


def pick_rows(ids, pieces, wide):
    total = sum(p.shape[0] for p in pieces)
    hot = (ids[...] == lax.broadcasted_iota(jnp.int32, (LANES, total), 1)).astype(F32).astype(BF16)
    for start, size in chunks(WIDE, 256):
        lanes = pl.ds(start, size)
        table = jnp.concatenate([p[:, lanes] for p in pieces], axis=0)
        wide[:, lanes] = dot(hot, table).astype(BF16)


def add_rows(ids, wide, pieces):
    total = sum(p.shape[0] for p in pieces)
    hot = (ids[...] == lax.broadcasted_iota(jnp.int32, (total, LANES), 0)).astype(F32).astype(BF16)
    for start, size in chunks(WIDE, 256):
        lanes = pl.ds(start, size)
        summed = dot(hot, wide[:, lanes]).astype(BF16)
        offset = 0
        for p in pieces:
            p[:, lanes] = summed[offset : offset + p.shape[0]]
            offset += p.shape[0]


def put_order(zero, one, two, g, degree, order, value):
    where, lead = {0: (zero, 0), 1: (one, 1), 2: (two, 2)}[abs(order)]
    base = LANES if order < 0 else 0
    where[pl.ds(base + GROUP * g, GROUP), pl.ds((degree - lead) * LANES, LANES)] = value


def forward_kernel(
    own, partner, far0, far1, far2, far3, src, tgt, turn, basis, w_rad,
    w0, w1r, w1i, w2r, w2i, back,
    agg0, agg1, agg2, agg3, pre, turned, outs,
    wide, zero, one, two, gated, rad,
):
    value = dot(basis[...], w_rad[...])
    pre[...] = value
    rad[...] = value * jax.nn.sigmoid(value)
    pick_rows(src, (own, partner, far0, far1, far2, far3), wide)

    def use(g, degree, order, part):
        rows = pl.ds(GROUP * g, GROUP)
        turned[rows, pl.ds(place_of(degree, order) * LANES, LANES)] = part
        put_order(zero, one, two, g, degree, order, (part * rad[rows, :]).astype(BF16))

    rotate(turn, wide, use)
    for start, size in chunks(7 * LANES, 256):
        outs[:, pl.ds(start, size)] = dot(zero[...], w0[:, pl.ds(start, size)])
    for stacked, real, imag, up, down, count in (
        (one, w1r, w1i, 7, 13, 6),
        (two, w2r, w2i, 19, 24, 5),
    ):
        for start, size in chunks(count * LANES, 256):
            a = dot(stacked[...], real[:, pl.ds(start, size)])
            b = dot(stacked[...], imag[:, pl.ds(start, size)])
            outs[:, pl.ds(up * LANES + start, size)] = a[:LANES] - b[LANES:]
            outs[:, pl.ds(down * LANES + start, size)] = a[LANES:] + b[:LANES]
    gate = jax.nn.sigmoid(outs[:, pl.ds(0, LANES)])
    for q in range(ORDERS):
        lanes = pl.ds(q * LANES, LANES)
        gated[:, lanes] = (outs[:, lanes] * gate).astype(BF16)
    rotate_back(back, gated, wide)
    add_rows(tgt, wide, (agg0, agg1, agg2, agg3))


def backward_kernel(
    up0, up1, up2, up3, tgt, src, turn, pre, w_rad,
    outs_far, w0_far, w1r_far, w1i_far, w2r_far, w2i_far, turned_far, back_far,
    own, partner, far0, far1, far2, far3, grad_basis,
    wide, zero, one, two, w0, w1r, w1i, w2r, w2i, back, turned, outs, grads, fragments, rad, sems,
):
    loads = copies(
        (outs_far, w0_far, w1r_far, w1i_far, w2r_far, w2i_far, turned_far, back_far),
        (outs, w0, w1r, w1i, w2r, w2i, turned, back),
        sems,
        0,
    )
    for c in loads:
        c.start()
    pick_rows(tgt, (up0, up1, up2, up3), wide)

    def use(g, degree, order, part):
        grads[pl.ds(GROUP * g, GROUP), pl.ds(place_of(degree, order) * LANES, LANES)] = part

    rotate(turn, wide, use)
    loads[0].wait()
    scalar = outs[:, pl.ds(0, LANES)]
    gate = jax.nn.sigmoid(scalar)
    slope = gate * (1.0 - gate)
    lead = grads[:, pl.ds(0, LANES)]
    weighted = lead * scalar
    for q in range(1, ORDERS):
        lanes = pl.ds(q * LANES, LANES)
        weighted = weighted + grads[:, lanes] * outs[:, lanes]
    zero[:, pl.ds(0, LANES)] = (
        lead * (gate + scalar * slope) + slope * (weighted - lead * scalar)
    ).astype(BF16)
    for stacked, count, base, q0 in ((zero, 6, 0, 1), (one, 6, 0, 7), (one, 6, LANES, 13), (two, 5, 0, 19), (two, 5, LANES, 24)):
        for k in range(count):
            value = (grads[:, pl.ds((q0 + k) * LANES, LANES)] * gate).astype(BF16)
            column = k + 1 if stacked is zero else k
            stacked[pl.ds(base, LANES), pl.ds(column * LANES, LANES)] = value
    value = pre[...]
    gate = jax.nn.sigmoid(value)
    rad[...] = value * gate
    slope = gate * (1.0 + value * (1.0 - gate))
    total = jnp.zeros((LANES, LANES), F32)

    def take(total, q, scaled):
        lanes = pl.ds(q * LANES, LANES)
        fragments[:, lanes] = (scaled * rad[...]).astype(BF16)
        return total + scaled * turned[:, lanes]

    for c in loads[1:7]:
        c.wait()
    for start, size in chunks(7 * LANES, 256):
        a = dot_nt(zero[...], w0[pl.ds(start, size), :])
        for k in range(size // LANES):
            total = take(total, start // LANES + k, a[:, k * LANES : (k + 1) * LANES])
    for stacked, real, imag, up, down, count in (
        (one, w1r, w1i, 7, 13, 6),
        (two, w2r, w2i, 19, 24, 5),
    ):
        for start, size in chunks(count * LANES, 256):
            a = dot_nt(stacked[...], real[pl.ds(start, size), :])
            b = dot_nt(stacked[...], imag[pl.ds(start, size), :])
            for k in range(size // LANES):
                cut = slice(k * LANES, (k + 1) * LANES)
                total = take(total, up + start // LANES + k, a[:LANES, cut] + b[LANES:, cut])
                total = take(total, down + start // LANES + k, a[LANES:, cut] - b[:LANES, cut])
    grad_basis[...] = dot_nt((total * slope).astype(BF16), w_rad[...])
    loads[7].wait()
    rotate_back(back, fragments, wide)
    add_rows(src, wide, (own, partner, far0, far1, far2, far3))


def kernel_call(kernel, near, far, outs, far_outs, scratch, flops, moved):
    inside, outside = pl.BlockSpec(memory_space=pltpu.VMEM), pl.BlockSpec(memory_space=pl.ANY)
    return pl.pallas_call(
        kernel,
        out_shape=outs + far_outs,
        in_specs=[inside] * near + [outside] * far,
        out_specs=(inside,) * len(outs) + (outside,) * len(far_outs),
        scratch_shapes=scratch,
        compiler_params=pltpu.CompilerParams(vmem_limit_bytes=VMEM),
        cost_estimate=pl.CostEstimate(flops=flops, bytes_accessed=moved, transcendentals=0),
    )


def shaped(*dims, kind=BF16):
    return jax.ShapeDtypeStruct(dims, kind)


def on_device(
    embeddings, species, species_gain, sources, targets, counts, send_left, send_right, rotations,
    radial_basis, weight_radial, weight_zero, weight_one_real, weight_one_imag, weight_two_real,
    weight_two_imag, cotangent,
):
    weights = (weight_zero, weight_one_real, weight_one_imag, weight_two_real, weight_two_imag)
    atoms = embeddings.shape[0]
    edges = sources.shape[0]
    blocks = lax.axis_size("space")
    member = lax.axis_index("edge")
    block = lax.axis_index("space")
    half, along = member // 4, member % 4
    odd = block % 2
    scale = (atoms / edges) ** 0.5

    def across(v):
        return lax.ppermute(v, "edge", [(s, (s + 4) % 8) for s in range(8)])

    def shift(v, k):
        return lax.ppermute(v, "edge", [(s, s // 4 * 4 + (s + k) % 4) for s in range(8)])

    def swap_near(v):
        return lax.ppermute(v, "space", [(b, b ^ 1) for b in range(blocks)])

    def swap_far(v):
        return lax.ppermute(v, "space", [(b, (b + 2 * (b % 2) - 1) % blocks) for b in range(blocks)])

    def after(*values):
        return lax.optimization_barrier(values)

    def spread(v):
        return [v] + [shift(v, 4 - d) for d in (1, 2, 3)]

    def collect(parts):
        total = parts[0].astype(F32)
        for d in (1, 2, 3):
            total = total + shift(parts[d], d).astype(F32)
        return total

    flat = embeddings.reshape(atoms, WIDE)
    halo = send_left.shape[1]
    lists = jnp.concatenate([send_left, send_right], axis=1).astype(BF16)
    lists = jnp.pad(lists, ((0, 2 * atoms - 1), (0, LANES - 2 * halo)))
    pair = jnp.concatenate([jnp.concatenate([flat, across(flat)], axis=0), lists], axis=1)
    gain = jnp.dot(
        (species[:, None] == lax.iota(jnp.int32, species_gain.shape[0])[None, :]).astype(F32),
        species_gain,
        precision=lax.Precision.HIGHEST,
    )
    upstream = (cotangent.astype(F32) * gain[:, None, :] * scale).astype(BF16).reshape(atoms, WIDE)
    up_far = across(upstream)
    pair, targets = after(pair, targets)
    far_pair = swap_far(pair)
    own_pieces = spread(pair)
    groups = LANES // GROUP
    turn, back = kernel_call(
        prep_kernel,
        1,
        1,
        (shaped(groups, TURN_ROWS, 256), shaped(groups, BACK_ROWS, 256)),
        (),
        [pltpu.VMEM((ROT_PAD, LANES), BF16)],
        2 * 10**9,
        6 * 10**6,
    )(rotations, pair)

    far_pair, back, sources = after(far_pair, back, sources)
    *own_pieces, back = after(*own_pieces, back)
    far_pieces = spread(far_pair)
    own_table = jnp.concatenate(own_pieces, axis=0)
    partner_table = swap_near(own_table)
    *far_pieces, up_far = after(*far_pieces, up_far)
    up_pair = jnp.concatenate([upstream, up_far], axis=0)
    up_pieces = spread(up_pair)

    def slot(atom):
        owner, row = atom // atoms, atom % atoms
        return (owner % 4 - along) % 4 * (2 * atoms) + (owner // 4 - half) % 2 * atoms + row

    near_lists = partner_table[0, WIDE : WIDE + 2 * halo].astype(jnp.int32)
    far_lists = far_pair[0, WIDE : WIDE + 2 * halo].astype(jnp.int32)
    on_odd = odd == 1
    lists = jnp.concatenate(
        [
            jnp.where(on_odd, near_lists, far_lists)[halo:],
            jnp.where(on_odd, far_lists, near_lists)[:halo],
        ]
    )
    block_atoms = 8 * atoms
    halo_hot = (sources[:, None] - block_atoms) == lax.iota(jnp.int32, 2 * halo)[None, :]
    halo_atom = jnp.sum(jnp.where(halo_hot, lists[None, :], 0), axis=1)
    on_left = sources < block_atoms + halo
    near = jnp.where(on_left, odd == 1, odd == 0)
    src = jnp.where(
        sources < block_atoms,
        slot(sources),
        jnp.where(near, block_atoms, 2 * block_atoms) + slot(halo_atom),
    ).astype(jnp.int32)
    live = member * edges + lax.iota(jnp.int32, edges) < counts[0]
    tgt = jnp.where(live, slot(targets), -1).astype(jnp.int32)
    src_col, src_row = src[:, None], src[None, :]
    tgt_col, tgt_row = tgt[:, None], tgt[None, :]

    def work():
        return [
            pltpu.VMEM((edges, WIDE), BF16),
            pltpu.VMEM((edges, 7 * LANES), BF16),
            pltpu.VMEM((2 * edges, 6 * LANES), BF16),
            pltpu.VMEM((2 * edges, 5 * LANES), BF16),
        ]

    piece = shaped(2 * atoms, WIDE)
    whole = shaped(block_atoms, WIDE)
    kept = shaped(edges, ORDERS * LANES, kind=F32)
    square = shaped(edges, LANES, kind=F32)
    *aggs, pre, turned, outs = kernel_call(
        forward_kernel,
        17,
        0,
        (piece, piece, piece, piece, square, kept, kept),
        (),
        work() + [pltpu.VMEM((edges, ORDERS * LANES), BF16), pltpu.VMEM((edges, LANES), F32)],
        4 * 10**9,
        20 * 10**6,
    )(
        own_table, partner_table, *far_pieces, src_col, tgt_row, turn, radial_basis, weight_radial,
        *weights, back,
    )

    agg_pair = collect(aggs)
    own_grad, near_grad, *far_grads, grad_basis = kernel_call(
        backward_kernel,
        9,
        8,
        (whole, whole, piece, piece, piece, piece, square),
        (),
        work()
        + [
            *[pltpu.VMEM(w.shape, BF16) for w in weights],
            pltpu.VMEM(back.shape, BF16),
            pltpu.VMEM((edges, ORDERS * LANES), F32),
            pltpu.VMEM((edges, ORDERS * LANES), F32),
            pltpu.VMEM((edges, ORDERS * LANES), F32),
            pltpu.VMEM((edges, ORDERS * LANES), BF16),
            pltpu.VMEM((edges, LANES), F32),
            pltpu.SemaphoreType.DMA((8,)),
        ],
        5 * 10**9,
        20 * 10**6,
    )(*up_pieces, tgt_col, src_row, turn, pre, weight_radial, outs, *weights, turned, back)

    *far_grads, near_grad, agg_pair = after(*far_grads, near_grad, agg_pair)
    near_home, agg_far = after(swap_near(near_grad), across(agg_pair[atoms:].astype(BF16)))
    aggregate = agg_pair[:atoms] + agg_far.astype(F32)
    updated = (
        embeddings.astype(F32) + gain[:, None, :] * scale * aggregate.reshape(embeddings.shape)
    ).astype(BF16)
    summed = own_grad.astype(F32) + near_home.astype(F32)
    parts = [summed[2 * atoms * d : 2 * atoms * (d + 1)].astype(BF16) for d in range(4)]
    *parts, far_sum = after(*parts, collect(far_grads).astype(BF16))
    grad_pair = collect(parts) + swap_far(far_sum).astype(F32)
    grad_rows = grad_pair[:atoms] + across(grad_pair[atoms:].astype(BF16)).astype(F32)
    grad_embeddings = cotangent.astype(F32) + grad_rows.reshape(cotangent.shape)
    return (updated, grad_embeddings, grad_basis)


def solution(mesh):
    both = ("space", "edge")
    placed = (
        P(both, None, None), P(both), P(), P(both), P(both), P("space"), P("space", None),
        P("space", None), P(None, both), P(both, None), P(), P(), P(), P(), P(), P(),
        P(both, None, None),
    )
    return jax.shard_map(
        on_device,
        mesh=mesh,
        in_specs=placed,
        out_specs=(P(both, None, None), P(both, None, None), P(both, None)),
        check_vma=False,
    )
```

```python
import jax
import jax.numpy as jnp
from jax import lax
from jax.experimental import pallas as pl
from jax.experimental.pallas import tpu as pltpu
from jax.sharding import PartitionSpec as P

F32 = jnp.float32
BF16 = jnp.bfloat16
LANES = 128
GROUP = 16
TOP = 6
COEFS = (TOP + 1) ** 2
ORDERS = 29
WIDE = COEFS * LANES
VMEM = 50 * 2**20

TILES = ((0, 1, 2, 3), (4,), (5,), (6,))


def place_of(degree, order):
    if order == 0:
        return degree
    start = {1: 7, -1: 13, 2: 19, -2: 24}[order]
    return start + degree - abs(order)


def tile_table():
    table = []
    row_start = 0
    for degrees in TILES:
        first = degrees[0] ** 2
        coefs = (degrees[-1] + 1) ** 2 - first
        pairs = [(d, m) for d in degrees for m in range(-min(d, 2), min(d, 2) + 1)]
        table.append((first, coefs, pairs, row_start))
        row_start += GROUP * len(pairs)
    return table, row_start


TABLE, TURN_ROWS = tile_table()
BACK_ROWS = GROUP * COEFS
ROT_ROWS = 235
ROT_PAD = 256


def selectors():
    row = lax.broadcasted_iota(jnp.int32, (8, ROT_PAD), 1)
    pair_all, coef_all, pair_tile, coef_tile = [jnp.full(row.shape, -1, jnp.int32) for _ in range(4)]
    offset = 0
    for degree in range(TOP + 1):
        cap, columns = min(degree, 2), 2 * degree + 1
        [(first, _, pairs, start)] = [e for e, d in zip(TABLE, TILES) if degree in d]
        for order in range(-cap, cap + 1):
            place = pairs.index((degree, order))
            inside = (row >= offset) & (row < offset + columns)
            coef = row - offset + degree * degree
            pair_all = jnp.where(inside, start // GROUP + place, pair_all)
            coef_all = jnp.where(inside, coef, coef_all)
            pair_tile = jnp.where(inside, place, pair_tile)
            coef_tile = jnp.where(inside, coef - first, coef_tile)
            offset += columns
    return pair_all[:1], coef_all[:1], pair_tile.astype(F32).T[:, :1], coef_tile.astype(F32).T[:, :1]


def dot(a, b):
    return jnp.dot(a, b, preferred_element_type=F32)


def dot_nt(a, b):
    return lax.dot_general(a, b, (((1,), (1,)), ((), ())), preferred_element_type=F32)


def chunks(total, size):
    return [(s, min(size, total - s)) for s in range(0, total, size)]


def copies(sources, places, sems, first):
    return [
        pltpu.make_async_copy(a, b, sems.at[first + k]) for k, (a, b) in enumerate(zip(sources, places))
    ]


def prep_kernel(rot, first, turn, back, rows_all):
    pair_all, coef_all, pair_tile, coef_tile = selectors()
    rows_all[...] = jnp.zeros_like(rows_all)
    rows_all[pl.ds(0, ROT_ROWS), :] = rot[...]
    row = lax.broadcasted_iota(jnp.int32, (LANES, 256), 0)
    lane = lax.broadcasted_iota(jnp.int32, (LANES, 256), 1) & (GROUP - 1)

    def keep(rows):
        r = lax.broadcasted_iota(jnp.int32, (rows, 256), 0) & (GROUP - 1)
        c = lax.broadcasted_iota(jnp.int32, (rows, 256), 1) & (GROUP - 1)
        return r == c

    def pick(rows, ids):
        group = lax.broadcasted_iota(jnp.int32, (rows, ROT_PAD), 0) // GROUP
        return (group == ids).astype(F32).astype(BF16)

    def mask(ids):
        return lax.broadcasted_iota(jnp.int32, (ROT_PAD, 256), 1) // GROUP == ids.astype(jnp.int32)

    work = (
        (mask(coef_tile), pick(TURN_ROWS, pair_all), keep(TURN_ROWS), turn),
        (mask(pair_tile), pick(BACK_ROWS, coef_all), keep(BACK_ROWS), back),
    )
    for g in range(LANES // GROUP):
        spread = (row == lane + GROUP * g).astype(F32).astype(BF16)
        laid = dot(rows_all[...], spread)
        for masked, picked, kept, out in work:
            full = dot(picked, jnp.where(masked, laid, 0.0).astype(BF16))
            out[g] = jnp.where(kept, full, 0.0).astype(BF16)


def rotate(turn, wide, use):
    for g in range(LANES // GROUP):
        rows = pl.ds(GROUP * g, GROUP)
        for first, coefs, pairs, start in TABLE:
            window = jnp.concatenate(
                [wide[rows, pl.ds((first + c) * LANES, LANES)] for c in range(coefs)], axis=0
            )
            block = turn[g, pl.ds(start, GROUP * len(pairs)), pl.ds(0, GROUP * coefs)]
            result = dot(block, window)
            for k, (degree, order) in enumerate(pairs):
                use(g, degree, order, result[GROUP * k : GROUP * (k + 1)])


def rotate_back(back, fragments, wide):
    for g in range(LANES // GROUP):
        rows = pl.ds(GROUP * g, GROUP)
        for first, coefs, pairs, _ in TABLE:
            window = jnp.concatenate(
                [fragments[rows, pl.ds(place_of(*p) * LANES, LANES)] for p in pairs], axis=0
            )
            block = back[g, pl.ds(GROUP * first, GROUP * coefs), pl.ds(0, GROUP * len(pairs))]
            result = dot(block, window)
            for c in range(coefs):
                wide[rows, pl.ds((first + c) * LANES, LANES)] = result[
                    GROUP * c : GROUP * (c + 1)
                ].astype(BF16)


def pick_rows(ids, pieces, wide):
    total = sum(p.shape[0] for p in pieces)
    hot = (ids[...] == lax.broadcasted_iota(jnp.int32, (LANES, total), 1)).astype(F32).astype(BF16)
    for start, size in chunks(WIDE, 256):
        lanes = pl.ds(start, size)
        table = jnp.concatenate([p[:, lanes] for p in pieces], axis=0)
        wide[:, lanes] = dot(hot, table).astype(BF16)


def add_rows(ids, wide, pieces):
    total = sum(p.shape[0] for p in pieces)
    hot = (ids[...] == lax.broadcasted_iota(jnp.int32, (total, LANES), 0)).astype(F32).astype(BF16)
    for start, size in chunks(WIDE, 256):
        lanes = pl.ds(start, size)
        summed = dot(hot, wide[:, lanes]).astype(BF16)
        offset = 0
        for p in pieces:
            p[:, lanes] = summed[offset : offset + p.shape[0]]
            offset += p.shape[0]


def put_order(zero, one, two, g, degree, order, value):
    where, lead = {0: (zero, 0), 1: (one, 1), 2: (two, 2)}[abs(order)]
    base = LANES if order < 0 else 0
    where[pl.ds(base + GROUP * g, GROUP), pl.ds((degree - lead) * LANES, LANES)] = value


def forward_kernel(
    own, partner, far0, far1, far2, far3, src, tgt, turn, basis, w_rad,
    w0, w1r, w1i, w2r, w2i, back,
    agg0, agg1, agg2, agg3, pre, turned, outs,
    wide, zero, one, two, gated, rad,
):
    value = dot(basis[...], w_rad[...])
    pre[...] = value
    rad[...] = value * jax.nn.sigmoid(value)
    pick_rows(src, (own, partner, far0, far1, far2, far3), wide)

    def use(g, degree, order, part):
        rows = pl.ds(GROUP * g, GROUP)
        turned[rows, pl.ds(place_of(degree, order) * LANES, LANES)] = part
        put_order(zero, one, two, g, degree, order, (part * rad[rows, :]).astype(BF16))

    rotate(turn, wide, use)
    for start, size in chunks(7 * LANES, 256):
        outs[:, pl.ds(start, size)] = dot(zero[...], w0[:, pl.ds(start, size)])
    for stacked, real, imag, up, down, count in (
        (one, w1r, w1i, 7, 13, 6),
        (two, w2r, w2i, 19, 24, 5),
    ):
        for start, size in chunks(count * LANES, 256):
            a = dot(stacked[...], real[:, pl.ds(start, size)])
            b = dot(stacked[...], imag[:, pl.ds(start, size)])
            outs[:, pl.ds(up * LANES + start, size)] = a[:LANES] - b[LANES:]
            outs[:, pl.ds(down * LANES + start, size)] = a[LANES:] + b[:LANES]
    gate = jax.nn.sigmoid(outs[:, pl.ds(0, LANES)])
    for q in range(ORDERS):
        lanes = pl.ds(q * LANES, LANES)
        gated[:, lanes] = (outs[:, lanes] * gate).astype(BF16)
    rotate_back(back, gated, wide)
    add_rows(tgt, wide, (agg0, agg1, agg2, agg3))


def backward_kernel(
    up0, up1, up2, up3, tgt, src, turn, pre, w_rad,
    outs_far, w0_far, w1r_far, w1i_far, w2r_far, w2i_far, turned_far, back_far,
    own, partner, far0, far1, far2, far3, grad_basis,
    wide, zero, one, two, w0, w1r, w1i, w2r, w2i, back, turned, outs, grads, fragments, rad, sems,
):
    loads = copies(
        (outs_far, w0_far, w1r_far, w1i_far, w2r_far, w2i_far, turned_far, back_far),
        (outs, w0, w1r, w1i, w2r, w2i, turned, back),
        sems,
        0,
    )
    for c in loads:
        c.start()
    pick_rows(tgt, (up0, up1, up2, up3), wide)

    def use(g, degree, order, part):
        grads[pl.ds(GROUP * g, GROUP), pl.ds(place_of(degree, order) * LANES, LANES)] = part

    rotate(turn, wide, use)
    loads[0].wait()
    scalar = outs[:, pl.ds(0, LANES)]
    gate = jax.nn.sigmoid(scalar)
    slope = gate * (1.0 - gate)
    lead = grads[:, pl.ds(0, LANES)]
    weighted = lead * scalar
    for q in range(1, ORDERS):
        lanes = pl.ds(q * LANES, LANES)
        weighted = weighted + grads[:, lanes] * outs[:, lanes]
    zero[:, pl.ds(0, LANES)] = (
        lead * (gate + scalar * slope) + slope * (weighted - lead * scalar)
    ).astype(BF16)
    for stacked, count, base, q0 in ((zero, 6, 0, 1), (one, 6, 0, 7), (one, 6, LANES, 13), (two, 5, 0, 19), (two, 5, LANES, 24)):
        for k in range(count):
            value = (grads[:, pl.ds((q0 + k) * LANES, LANES)] * gate).astype(BF16)
            column = k + 1 if stacked is zero else k
            stacked[pl.ds(base, LANES), pl.ds(column * LANES, LANES)] = value
    value = pre[...]
    gate = jax.nn.sigmoid(value)
    rad[...] = value * gate
    slope = gate * (1.0 + value * (1.0 - gate))
    total = jnp.zeros((LANES, LANES), F32)

    def take(total, q, scaled):
        lanes = pl.ds(q * LANES, LANES)
        fragments[:, lanes] = (scaled * rad[...]).astype(BF16)
        return total + scaled * turned[:, lanes]

    for c in loads[1:7]:
        c.wait()
    for start, size in chunks(7 * LANES, 256):
        a = dot_nt(zero[...], w0[pl.ds(start, size), :])
        for k in range(size // LANES):
            total = take(total, start // LANES + k, a[:, k * LANES : (k + 1) * LANES])
    for stacked, real, imag, up, down, count in (
        (one, w1r, w1i, 7, 13, 6),
        (two, w2r, w2i, 19, 24, 5),
    ):
        for start, size in chunks(count * LANES, 256):
            a = dot_nt(stacked[...], real[pl.ds(start, size), :])
            b = dot_nt(stacked[...], imag[pl.ds(start, size), :])
            for k in range(size // LANES):
                cut = slice(k * LANES, (k + 1) * LANES)
                total = take(total, up + start // LANES + k, a[:LANES, cut] + b[LANES:, cut])
                total = take(total, down + start // LANES + k, a[LANES:, cut] - b[:LANES, cut])
    grad_basis[...] = dot_nt((total * slope).astype(BF16), w_rad[...])
    loads[7].wait()
    rotate_back(back, fragments, wide)
    add_rows(src, wide, (own, partner, far0, far1, far2, far3))


def kernel_call(kernel, near, far, outs, far_outs, scratch, flops, moved):
    inside, outside = pl.BlockSpec(memory_space=pltpu.VMEM), pl.BlockSpec(memory_space=pl.ANY)
    return pl.pallas_call(
        kernel,
        out_shape=outs + far_outs,
        in_specs=[inside] * near + [outside] * far,
        out_specs=(inside,) * len(outs) + (outside,) * len(far_outs),
        scratch_shapes=scratch,
        compiler_params=pltpu.CompilerParams(vmem_limit_bytes=VMEM),
        cost_estimate=pl.CostEstimate(flops=flops, bytes_accessed=moved, transcendentals=0),
    )


def shaped(*dims, kind=BF16):
    return jax.ShapeDtypeStruct(dims, kind)


def on_device(
    embeddings, species, species_gain, sources, targets, counts, send_left, send_right, rotations,
    radial_basis, weight_radial, weight_zero, weight_one_real, weight_one_imag, weight_two_real,
    weight_two_imag, cotangent,
):
    weights = (weight_zero, weight_one_real, weight_one_imag, weight_two_real, weight_two_imag)
    atoms = embeddings.shape[0]
    edges = sources.shape[0]
    blocks = lax.axis_size("space")
    member = lax.axis_index("edge")
    block = lax.axis_index("space")
    half, along = member // 4, member % 4
    odd = block % 2
    scale = (atoms / edges) ** 0.5

    def across(v):
        return lax.ppermute(v, "edge", [(s, (s + 4) % 8) for s in range(8)])

    def shift(v, k):
        return lax.ppermute(v, "edge", [(s, s // 4 * 4 + (s + k) % 4) for s in range(8)])

    def swap_near(v):
        return lax.ppermute(v, "space", [(b, b ^ 1) for b in range(blocks)])

    def swap_far(v):
        return lax.ppermute(v, "space", [(b, (b + 2 * (b % 2) - 1) % blocks) for b in range(blocks)])

    def after(*values):
        return lax.optimization_barrier(values)

    def spread(v):
        return [v] + [shift(v, 4 - d) for d in (1, 2, 3)]

    def collect(parts):
        total = parts[0].astype(F32)
        for d in (1, 2, 3):
            total = total + shift(parts[d], d).astype(F32)
        return total

    flat = embeddings.reshape(atoms, WIDE)
    halo = send_left.shape[1]
    lists = jnp.concatenate([send_left, send_right], axis=1)
    lists = jnp.pad(lists, ((0, 2 * atoms - 1), (0, LANES - 2 * halo))).astype(BF16)
    pair = jnp.concatenate([jnp.concatenate([flat, across(flat)], axis=0), lists], axis=1)
    gain = jnp.dot(
        (species[:, None] == lax.iota(jnp.int32, species_gain.shape[0])[None, :]).astype(F32),
        species_gain,
        precision=lax.Precision.HIGHEST,
    )
    upstream = (cotangent.astype(F32) * gain[:, None, :] * scale).astype(BF16).reshape(atoms, WIDE)
    up_far = across(upstream)
    pair, targets = after(pair, targets)
    far_pair = swap_far(pair)
    own_pieces = spread(pair)
    groups = LANES // GROUP
    turn, back = kernel_call(
        prep_kernel,
        1,
        1,
        (shaped(groups, TURN_ROWS, 256), shaped(groups, BACK_ROWS, 256)),
        (),
        [pltpu.VMEM((ROT_PAD, LANES), BF16)],
        2 * 10**9,
        6 * 10**6,
    )(rotations, pair)

    far_pair, back, sources = after(far_pair, back, sources)
    *own_pieces, back = after(*own_pieces, back)
    far_pieces = spread(far_pair)
    own_table = jnp.concatenate(own_pieces, axis=0)
    partner_table = swap_near(own_table)
    *far_pieces, up_far = after(*far_pieces, up_far)
    up_pair = jnp.concatenate([upstream, up_far], axis=0)
    up_pieces = spread(up_pair)

    def slot(atom):
        owner, row = atom // atoms, atom % atoms
        return (owner % 4 - along) % 4 * (2 * atoms) + (owner // 4 - half) % 2 * atoms + row

    near_lists = partner_table[0, WIDE : WIDE + 2 * halo].astype(jnp.int32)
    far_lists = far_pair[0, WIDE : WIDE + 2 * halo].astype(jnp.int32)
    on_odd = odd == 1
    lists = jnp.concatenate(
        [
            jnp.where(on_odd, near_lists, far_lists)[halo:],
            jnp.where(on_odd, far_lists, near_lists)[:halo],
        ]
    )
    block_atoms = 8 * atoms
    halo_hot = (sources[:, None] - block_atoms) == lax.iota(jnp.int32, 2 * halo)[None, :]
    halo_atom = jnp.sum(jnp.where(halo_hot, lists[None, :], 0), axis=1)
    on_left = sources < block_atoms + halo
    near = jnp.where(on_left, odd == 1, odd == 0)
    src = jnp.where(
        sources < block_atoms,
        slot(sources),
        jnp.where(near, block_atoms, 2 * block_atoms) + slot(halo_atom),
    ).astype(jnp.int32)
    live = member * edges + lax.iota(jnp.int32, edges) < counts[0]
    tgt = jnp.where(live, slot(targets), -1).astype(jnp.int32)
    src_col, src_row = src[:, None], src[None, :]
    tgt_col, tgt_row = tgt[:, None], tgt[None, :]

    def work():
        return [
            pltpu.VMEM((edges, WIDE), BF16),
            pltpu.VMEM((edges, 7 * LANES), BF16),
            pltpu.VMEM((2 * edges, 6 * LANES), BF16),
            pltpu.VMEM((2 * edges, 5 * LANES), BF16),
        ]

    piece = shaped(2 * atoms, WIDE)
    whole = shaped(block_atoms, WIDE)
    kept = shaped(edges, ORDERS * LANES, kind=F32)
    square = shaped(edges, LANES, kind=F32)
    *aggs, pre, turned, outs = kernel_call(
        forward_kernel,
        17,
        0,
        (piece, piece, piece, piece, square, kept, kept),
        (),
        work() + [pltpu.VMEM((edges, ORDERS * LANES), BF16), pltpu.VMEM((edges, LANES), F32)],
        4 * 10**9,
        20 * 10**6,
    )(
        own_table, partner_table, *far_pieces, src_col, tgt_row, turn, radial_basis, weight_radial,
        *weights, back,
    )

    agg_pair = collect(aggs)
    own_grad, near_grad, *far_grads, grad_basis = kernel_call(
        backward_kernel,
        9,
        8,
        (whole, whole, piece, piece, piece, piece, square),
        (),
        work()
        + [
            *[pltpu.VMEM(w.shape, BF16) for w in weights],
            pltpu.VMEM(back.shape, BF16),
            pltpu.VMEM((edges, ORDERS * LANES), F32),
            pltpu.VMEM((edges, ORDERS * LANES), F32),
            pltpu.VMEM((edges, ORDERS * LANES), F32),
            pltpu.VMEM((edges, ORDERS * LANES), BF16),
            pltpu.VMEM((edges, LANES), F32),
            pltpu.SemaphoreType.DMA((8,)),
        ],
        5 * 10**9,
        20 * 10**6,
    )(*up_pieces, tgt_col, src_row, turn, pre, weight_radial, outs, *weights, turned, back)

    *far_grads, near_grad, agg_pair = after(*far_grads, near_grad, agg_pair)
    near_home, agg_far = swap_near(near_grad), across(agg_pair[atoms:].astype(BF16))
    aggregate = agg_pair[:atoms] + agg_far.astype(F32)
    updated = (
        embeddings.astype(F32) + gain[:, None, :] * scale * aggregate.reshape(embeddings.shape)
    ).astype(BF16)
    summed = own_grad.astype(F32) + near_home.astype(F32)
    parts = [summed[2 * atoms * d : 2 * atoms * (d + 1)].astype(BF16) for d in range(4)]
    *parts, far_sum = after(*parts, collect(far_grads).astype(BF16))
    grad_pair = collect(parts) + swap_far(far_sum).astype(F32)
    grad_rows = grad_pair[:atoms] + across(grad_pair[atoms:].astype(BF16)).astype(F32)
    grad_embeddings = cotangent.astype(F32) + grad_rows.reshape(cotangent.shape)
    return (updated, grad_embeddings, grad_basis)


def solution(mesh):
    both = ("space", "edge")
    placed = (
        P(both, None, None), P(both), P(), P(both), P(both), P("space"), P("space", None),
        P("space", None), P(None, both), P(both, None), P(), P(), P(), P(), P(), P(),
        P(both, None, None),
    )
    return jax.shard_map(
        on_device,
        mesh=mesh,
        in_specs=placed,
        out_specs=(P(both, None, None), P(both, None, None), P(both, None)),
        check_vma=False,
    )
```
